32 devices in a mesh: dp: 8 (over z, core), ctx: 4 (over y, x).
Axes of the slice: x: 2, y: 2, z: 4, core: 2. Of those that a mesh axis runs over, the one named last changes fastest.
Arguments:
- queries: bfloat16 [8, 1536, 1024], P('dp', 'ctx'), may hold values from -32 to 32
- keys: bfloat16 [8, 1536, 1024], P('dp', 'ctx'), may hold values from -32 to 32
- values: bfloat16 [8, 1536, 1024], P('dp', 'ctx'), may hold values from -6 to 6
- out_weight: bfloat16 [2048, 1024], replicated, may hold values from -0.1875 to 0.1875
- out_cot: bfloat16 [8, 1536, 2048], P('dp', 'ctx'), may hold values from -6 to 6
- block_list: int32 [12, 8], replicated, may hold values from 0 to 11, as said below
Outputs:
- attended: bfloat16 [8, 1536, 2048], P('dp', 'ctx')
- query_gradient: bfloat16 [8, 1536, 1024], P('dp', 'ctx')
- key_grad: bfloat16 [8, 1536, 1024], P('dp', 'ctx')
- value_grad: bfloat16 [8, 1536, 1024], P('dp', 'ctx')
- weight_grad: float32 [2048, 1024], P(('dp', 'ctx'))
The draws below stay inside these ranges and needn't reach their ends.
Inputs may be any that keep to these rules, and one draw needn't show every extreme that they name: `block_list`: row i names 8 different blocks: i - 1, i and i + 1 modulo 12, then the 2 global blocks (the same in every row) where they are not among those three, then other blocks at random.
All inputs are finite; a program needn't handle non-finite values.
Results may differ from the reference program's by a relative error of at most 0.015.
Values may be sent and summed in bfloat16 or wider, within the bound.
A program may use at most 128 MiB of HBM per device.

```python
import math
import jax
import jax.numpy as jnp
from jax import lax

D = 2048
HEADS = 8
HEAD_SIZE = 128
BLOCK_TOKENS = 128
CHOSEN_BLOCKS = 8
NGLOB = 2
HD = 1024
SEQ = 1536
NBLK = 12
N_DP = 8


def drawn_pair(key):
    full_shape = (N_DP, SEQ, HD)
    base_query = jax.random.normal(jax.random.fold_in(key, 11), full_shape, jnp.float32)
    base_key = jax.random.normal(jax.random.fold_in(key, 12), full_shape, jnp.float32)
    return (1.4 * jnp.clip(base_query, -6.0, 6.0), 1.4 * jnp.clip(base_key, -6.0, 6.0))


def draw_queries(key, part):
    return drawn_pair(key)[0].astype(jnp.bfloat16)


def draw_keys(key, part):
    return drawn_pair(key)[1].astype(jnp.bfloat16)


def draw_block_list(key, part):
    rows_idx = jnp.arange(NBLK, dtype=jnp.int32)[:, None]
    cols_idx = jnp.arange(NBLK, dtype=jnp.int32)[None, :]
    glob_score = jax.random.randint(jax.random.fold_in(key, 21), (NBLK,), 0, 1 << 16, dtype=jnp.int32) * NBLK + jnp.arange(NBLK, dtype=jnp.int32)
    unused_vals, global_ids = lax.top_k(glob_score, NGLOB)
    is_global = jnp.any(jnp.arange(NBLK, dtype=jnp.int32)[:, None] == global_ids[None, :], axis=1).astype(jnp.int32)
    priority = jax.random.randint(jax.random.fold_in(key, 22), (NBLK, NBLK), 0, 1 << 12, dtype=jnp.int32) * NBLK + cols_idx + is_global[None, :] * (1 << 22)
    offset = (cols_idx - rows_idx) % NBLK
    in_window = (offset == 0) | (offset == 1) | (offset == NBLK - 1)
    priority = jnp.where(in_window, -1, priority)
    unused_top, picked = lax.top_k(priority, CHOSEN_BLOCKS - 3)
    window = jnp.concatenate([(rows_idx - 1) % NBLK, rows_idx, (rows_idx + 1) % NBLK], axis=1)
    return jnp.concatenate([window, picked.astype(jnp.int32)], axis=1).astype(jnp.int32)


def levels(stream_key, dims, shards, low, high):
    factor_of, own = 1.0, jax.random.fold_in(stream_key, 6)
    for dim, parts in shards:
        draws = jnp.exp(jax.random.uniform(jax.random.fold_in(own, dim), (parts,), jnp.float32, low / len(shards), high / len(shards)))
        factor_of = factor_of * jnp.repeat(draws, dims[dim] // parts).reshape([-1 if axis == dim else 1 for axis in range(len(dims))])
    return factor_of


def normal_values(own_key, dims, spread, reach, pieces=(), held_as=jnp.bfloat16):
    result = jax.random.normal(own_key, dims, jnp.float32) * spread
    if len(pieces) > 0:
        result = levels(own_key, dims, pieces, -0.22, 0.18) * result
    return jnp.clip(result, min=-reach, max=reach).astype(held_as)


def setup_inputs(seed: int = 0) -> dict:
    arg_keys = jax.random.split(jax.random.key(seed), 7)
    queries = draw_queries(jax.random.fold_in(arg_keys[6], 71), 0)
    keys = draw_keys(jax.random.fold_in(arg_keys[6], 71), 0)
    values = normal_values(arg_keys[2], (N_DP, SEQ, HD), 1.0, 6.0, ((0, 8), (1, 4)))
    out_weight = normal_values(arg_keys[3], (D, HD), HD ** -0.5, 0.1875)
    out_cot = normal_values(arg_keys[4], (N_DP, SEQ, D), 1.0, 6.0, ((0, 8), (1, 4)))
    block_list = draw_block_list(jax.random.fold_in(arg_keys[6], 71), 0)
    return {"queries": queries, "keys": keys, "values": values, "out_weight": out_weight, "out_cot": out_cot, "block_list": block_list}


def select_rows(source_table, block_list):
    block_total = block_list.shape[0]
    gathered = source_table[block_list.reshape(-1)]
    return gathered.reshape(block_total, CHOSEN_BLOCKS * BLOCK_TOKENS, HEAD_SIZE)

def head_pass(query_head, key_head, value_head, cot_head, block_list):
    block_total = block_list.shape[0]
    inverse_root_scale = 1.0 / math.sqrt(HEAD_SIZE)
    blocked_queries = query_head.reshape(block_total, BLOCK_TOKENS, HEAD_SIZE).astype(jnp.float32)
    chosen_keys = select_rows(key_head.reshape(block_total, BLOCK_TOKENS, HEAD_SIZE), block_list).astype(jnp.float32)
    chosen_values = select_rows(value_head.reshape(block_total, BLOCK_TOKENS, HEAD_SIZE), block_list).astype(jnp.float32)
    logit_scores = jnp.einsum('vht,vrt->vhr', blocked_queries, chosen_keys) * inverse_root_scale
    row_max = lax.optimization_barrier(jnp.max(logit_scores, axis=-1, keepdims=True))
    expo_rows = jnp.exp(logit_scores - row_max)
    row_sum = lax.optimization_barrier(jnp.sum(expo_rows, axis=-1, keepdims=True))
    log_total = row_max + jnp.log(row_sum)
    weight_matrix = (expo_rows / row_sum).astype(jnp.bfloat16)
    attention_probs = jnp.einsum('ysl,yli->ysi', weight_matrix.astype(jnp.float32), chosen_values).astype(jnp.bfloat16)
    cotangent_block_rows = cot_head.reshape(block_total, BLOCK_TOKENS, HEAD_SIZE).astype(jnp.float32)
    row_dot = lax.optimization_barrier(jnp.sum(cotangent_block_rows * attention_probs.astype(jnp.float32), axis=-1))
    probs = jnp.exp(logit_scores - log_total)
    probs_narrow = probs.astype(jnp.bfloat16).astype(jnp.float32)
    flat_picks = block_list.reshape(-1).astype(jnp.int32)
    value_grad_terms = jnp.einsum('lgh,lga->lha', probs_narrow, cotangent_block_rows).reshape(block_total * CHOSEN_BLOCKS, BLOCK_TOKENS, HEAD_SIZE)
    value_acc = jnp.zeros((block_total, BLOCK_TOKENS, HEAD_SIZE), jnp.float32).at[flat_picks].add(value_grad_terms)
    cotangent_probs = jnp.einsum('vht,vrt->vhr', cotangent_block_rows, chosen_values)
    score_cotangent = (probs * (cotangent_probs - row_dot[..., None])).astype(jnp.bfloat16).astype(jnp.float32)
    query_gradient = (jnp.einsum('ysl,yli->ysi', score_cotangent, chosen_keys) * inverse_root_scale).astype(jnp.bfloat16)
    key_grad_terms = jnp.einsum('lgh,lga->lha', score_cotangent, blocked_queries).reshape(block_total * CHOSEN_BLOCKS, BLOCK_TOKENS, HEAD_SIZE)
    key_acc = jnp.zeros((block_total, BLOCK_TOKENS, HEAD_SIZE), jnp.float32).at[flat_picks].add(key_grad_terms)
    key_grad = (key_acc * inverse_root_scale).astype(jnp.bfloat16)
    value_grad = value_acc.astype(jnp.bfloat16)
    return (attention_probs.reshape(SEQ, HEAD_SIZE), query_gradient.reshape(SEQ, HEAD_SIZE), key_grad.reshape(SEQ, HEAD_SIZE), value_grad.reshape(SEQ, HEAD_SIZE))

def split_heads(matrix):
    return matrix.reshape(SEQ, HEADS, HEAD_SIZE).transpose(1, 0, 2)

def join_heads(stacked):
    return stacked.transpose(1, 0, 2).reshape(SEQ, HD)

def reference(queries, keys, values, out_weight, out_cot, block_list):

    def replica(running, inputs):
        query_rows, key_rows, value_rows, cot_rows = inputs
        attn_cot = jnp.dot(cot_rows, out_weight, preferred_element_type=jnp.float32).astype(jnp.bfloat16)

        def one_head(packed):
            return head_pass(packed[0], packed[1], packed[2], packed[3], block_list)
        results = lax.map(one_head, (split_heads(query_rows), split_heads(key_rows), split_heads(value_rows), split_heads(attn_cot)))
        attention_probs = join_heads(results[0])
        attended = jnp.dot(attention_probs, out_weight.T, preferred_element_type=jnp.float32).astype(jnp.bfloat16)
        weight_term = jnp.dot(cot_rows.T, attention_probs, preferred_element_type=jnp.float32)
        outputs = (attended, join_heads(results[1]), join_heads(results[2]), join_heads(results[3]))
        return (running + weight_term, outputs)
    start_sum = jnp.zeros((D, HD), jnp.float32)
    weight_sum, stacked = lax.scan(replica, start_sum, (queries, keys, values, out_cot))
    weight_grad = weight_sum / N_DP
    return (stacked[0], stacked[1], stacked[2], stacked[3], weight_grad)
```

```python
import functools
import math

import jax
import jax.numpy as jnp
from jax import lax
from jax.experimental import pallas as pl
from jax.experimental.pallas import tpu as pltpu
from jax.sharding import PartitionSpec as P

HEAD_SIZE = 128
BLOCK_TOKENS = 128
MESH = pl.DeviceIdType.MESH
BF16 = jnp.bfloat16
F32 = jnp.float32
VMEM_BYTES = 60 * 1024 * 1024


def mm(a, b, ca=1, cb=0):
    return lax.dot_general(a, b, (((ca,), (cb,)), ((), ())), preferred_element_type=F32)


def span(i, size):
    return pl.ds(pl.multiple_of(i * size, size), size)


def layer_kernel(n, nz, heads, names, picks, q, k, v, w, oc, out, dqo, dko, dvo, wg, *scratch):
    r = dict(zip(names, scratch))
    me = lax.axis_index("ctx")
    dp = lax.axis_index("dp")
    core = lax.rem(dp, 2)
    other = dp + 1 - 2 * core
    z = dp // 2
    held = q.shape[0]
    tokens = held * BLOCK_TOKENS
    model = w.shape[0]
    chosen, blocks = picks.shape
    sub = wg.shape[0]
    empty = blocks * chosen
    scale = 1.0 / math.sqrt(HEAD_SIZE)
    factor = scale * math.log2(math.e)
    ocv, octv, wv, seq = r["ocv"], r["octv"], r["wv"], r["seq"]
    acc, ps, dss, kt, vt = r["acc"], r["ps"], r["dss"], r["kt"], r["vt"]
    pos, loc = r["pos"], r["loc"]

    barrier = pltpu.get_barrier_semaphore()
    up = lax.rem(z + 1, nz) * 2 + core
    down = lax.rem(z + nz - 1, nz) * 2 + core
    for d in range(1, n):
        pl.semaphore_signal(
            barrier, inc=1, device_id=(dp, lax.rem(me + d, n)), device_id_type=MESH
        )
    for target in (other, up, down):
        pl.semaphore_signal(barrier, inc=1, device_id=(target, me), device_id_type=MESH)
    pl.semaphore_wait(barrier, n - 1 + 3)

    def partner(d):
        return lax.rem(me + d, n)

    def column(p, h):
        return span(p * heads + h, HEAD_SIZE)

    mine = pl.ds(me * held, held)

    class Trade:
        def __init__(self, src_of, dst, sems, where):
            self.src_of, self.dst = src_of, dst
            self.send, self.recv, self.own_sem = (r[sems + x].at[where] for x in "srl")

        def copy(self, d):
            p = partner(d)
            return pltpu.make_async_remote_copy(
                self.src_of(p), self.dst, self.send.at[d], self.recv.at[d],
                device_id=(dp, p), device_id_type=MESH,
            )

        def own(self):
            return pltpu.make_async_copy(self.src_of(me), self.dst, self.own_sem)

        def start(self):
            for d in range(1, n):
                self.copy(d).start()
            self.own().start()

        def arrive(self):
            self.own().wait()
            for d in range(1, n):
                self.copy(d).wait_recv()

        def sent(self):
            for d in range(1, n):
                self.copy(d).wait_send()

    rows = {
        (t, h): Trade(lambda p, x=x, h=h: x.at[:, :, column(p, h)], r[f"{t}{h}"].at[mine], "in_", (h, i))
        for i, (t, x) in enumerate((("k", k), ("q", q), ("v", v)))
        for h in range(heads)
    }
    cots = [
        Trade(lambda p, h=h: r["cotbuf"].at[h, p], r[f"c{h}"].at[mine], "in_", (h, 3))
        for h in range(heads)
    ]
    attns = [
        Trade(
            lambda p, h=h: r["attn"].at[h, span(p, tokens), :],
            seq.at[h, :, span(me, HEAD_SIZE)], "out_", (h, 0),
        )
        for h in range(heads)
    ]
    grads = {
        (t, h): Trade(
            lambda p, h=h, t=t: r[t].at[h, span(p, tokens), :], o.at[:, column(me, h)], "out_", (h, i)
        )
        for i, t, o in ((1, "dq", dqo), (2, "dk", dko), (3, "dv", dvo))
        for h in range(heads)
    }

    for h in range(heads):
        for t in "kqv":
            rows[t, h].start()
    load_oc = pltpu.make_async_copy(oc, ocv, loc.at[0])
    load_oc.start()
    load_w = []
    for h in range(heads):
        for p in range(n):
            copy = pltpu.make_async_copy(
                w.at[:, pl.ds((p * heads + h) * HEAD_SIZE, HEAD_SIZE)],
                wv.at[h, :, pl.ds(p * HEAD_SIZE, HEAD_SIZE)],
                r["wsem"].at[h, p],
            )
            copy.start()
            load_w.append(copy)

    def place(i, carry):
        def one(b, carry):
            at = empty
            for j in range(chosen):
                at = jnp.where(picks[j, i] == b, i * chosen + j, at)
            pos[i, b] = at
            return carry

        return lax.fori_loop(0, blocks, one, carry)

    lax.fori_loop(0, blocks, place, 0)
    for h in range(heads):
        ps[h, empty] = jnp.zeros((BLOCK_TOKENS, BLOCK_TOKENS), BF16)
    dss[empty] = jnp.zeros((BLOCK_TOKENS, BLOCK_TOKENS), BF16)

    load_oc.wait()

    def flip(i, carry):
        octv[span(i, 256), :] = ocv[:, span(i, 256)].T
        return carry

    lax.fori_loop(0, model // 256, flip, 0)
    for copy in load_w:
        copy.wait()

    def work_cot(h):
        def body(p, carry):
            r["cotbuf"][h, p] = (
                mm(ocv[...], wv[h, :, span(p, HEAD_SIZE)])
                .astype(BF16)
                .reshape(held, BLOCK_TOKENS, HEAD_SIZE)
            )
            return carry

        lax.fori_loop(0, n, body, 0)

    for h in range(heads):
        work_cot(h)

    def listed(ref, i, axis):
        return jnp.concatenate([ref[picks[j, i]] for j in range(chosen)], axis=axis)

    def forward_block(h, i):
        st = mm(listed(r[f"k{h}"], i, 0), r[f"q{h}"][i], 1, 1)
        top = jnp.max(st, axis=0, keepdims=True)
        e = jnp.exp2((st - top) * factor)
        inv = 1.0 / jnp.sum(e, axis=0, keepdims=True)
        low = (e * inv).astype(BF16)
        a = mm(listed(vt, i, 1), low).astype(BF16)
        r["attn"][h, span(i, BLOCK_TOKENS), :] = a.T
        for j in range(chosen):
            ps[h, i * chosen + j] = low[j * BLOCK_TOKENS : (j + 1) * BLOCK_TOKENS]

    def backward_block(h, i):
        at = span(i, BLOCK_TOKENS)
        ci = r[f"c{h}"][i]
        dpt = mm(listed(r[f"v{h}"], i, 0), ci, 1, 1)
        dot = jnp.sum(
            (ci.astype(F32) * r["attn"][h, at, :].astype(F32)).T, axis=0, keepdims=True
        )
        parts = []
        for j in range(chosen):
            part = slice(j * BLOCK_TOKENS, (j + 1) * BLOCK_TOKENS)
            ds = (ps[h, i * chosen + j].astype(F32) * (dpt[part] - dot)).astype(BF16)
            dss[i * chosen + j] = ds
            parts.append(ds)
        r["dq"][h, at, :] = (mm(listed(kt, i, 1), jnp.concatenate(parts, axis=0)) * scale).T.astype(BF16)

    def collect_part(h, p):
        def wide(kept):
            return jnp.concatenate(
                [
                    jnp.concatenate([kept(pos[i, p * held + x]) for i in range(blocks)], axis=1)
                    for x in range(held)
                ],
                axis=0,
            )

        at = span(p, tokens)
        pst = wide(lambda slot: ps[h, slot])
        r["dv"][h, at, :] = mm(pst, r[f"c{h}"][...].reshape(-1, HEAD_SIZE)).astype(BF16)
        dst = wide(lambda slot: dss[slot])
        r["dk"][h, at, :] = (mm(dst, r[f"q{h}"][...].reshape(-1, HEAD_SIZE)) * scale).astype(BF16)

    def turn(src, dst):
        def body(b, carry):
            dst[b] = src[b].T
            return carry

        lax.fori_loop(0, blocks, body, 0)

    def by_partner(work, trades, hooks):
        def body(t, carry):
            d = t + 1
            work(partner(d))

            @pl.when(d < n)
            def _():
                for trade in trades:
                    trade.copy(d).start()

            for at, hook in hooks.items():
                pl.when(t == at)(hook)
            return carry

        lax.fori_loop(0, n, body, 0)
        for trade in trades:
            trade.own().start()

    def forward(h):
        for t in "kqv":
            rows[t, h].arrive()
        turn(r[f"v{h}"], vt)

        def work(p):
            for x in range(held):
                forward_block(h, p * held + x)

        by_partner(work, [attns[h]], {})

    def backward(h, hooks):
        turn(r[f"k{h}"], kt)
        cots[h].arrive()

        def work(p):
            for x in range(held):
                backward_block(h, p * held + x)

        by_partner(work, [grads["dq", h]], hooks)

    def collect(h, hooks):
        by_partner(lambda p: collect_part(h, p), [grads["dv", h], grads["dk", h]], hooks)

    def term(h, c, who):
        return mm(octv[span(2 * c + who, n * sub), :], seq[h]).reshape(n, sub, -1)

    def core_copy(h, c):
        return pltpu.make_async_remote_copy(
            r["csend"].at[h, c], r["crecv"].at[h, c], r["csem_s"].at[h, c], r["csem_r"].at[h, c],
            device_id=(other, me), device_id_type=MESH,
        )

    def give(h):
        def body(c, carry):
            r["csend"][h, c] = term(h, c, 1 - core).astype(BF16)
            core_copy(h, c).start()
            return carry

        lax.fori_loop(0, nz, body, 0)

        def keep(c, carry):
            acc[h, c] = term(h, c, core)
            return carry

        lax.fori_loop(0, nz, keep, 0)

    def take(h):
        def body(c, carry):
            core_copy(h, c).wait()
            for s in range(n):
                acc[h, c, s] += r["crecv"][h, c, s].astype(F32)
            return carry

        lax.fori_loop(0, nz, body, 0)

    def hop(h, c, s, buf, sem, target):
        return pltpu.make_async_remote_copy(
            r["zsend"].at[h, c, s], r[buf].at[h, c, s], r["zsem"].at[h, c, s],
            r[sem].at[h, c, s], device_id=(target, me), device_id_type=MESH,
        )

    def right(h, c, s):
        return hop(h, c, s, "rrecv", "rsem", up)

    def left(h, c, s):
        return hop(h, c, s, "lrecv", "lsem", down)

    def burst(h, b):
        def one_way(rank, chunk_of, link, buf):
            count = jnp.where(rank == 0, nz - 1 if b == 0 else 0, jnp.where(rank <= b, 1, 0))

            def body(i, carry):
                c = chunk_of(b - rank + i // n)
                s = lax.rem(i, n)

                @pl.when(rank > 0)
                def _():
                    link(h, c, s).wait_recv()
                    acc[h, c, s] += r[buf][h, c, s].astype(F32)

                r["zsend"][h, c, s] = acc[h, c, s].astype(BF16)
                link(h, c, s).start()
                return carry

            lax.fori_loop(0, count * n, body, 0)

        one_way(z, lambda x: nz - 1 - x, right, "rrecv")
        one_way(nz - 1 - z, lambda x: x, left, "lrecv")

    def cross(h, s, slot):
        return pltpu.make_async_remote_copy(
            r["xsend"].at[h, s], r["xrecv"].at[h, slot], r["xsem_s"].at[h, s],
            r["xsem_r"].at[h, slot], device_id=(dp, s), device_id_type=MESH,
        )

    def finish(h):
        def body(s, carry):
            @pl.when(z > 0)
            def _():
                right(h, z, s).wait_recv()
                acc[h, z, s] += r["rrecv"][h, z, s].astype(F32)

            @pl.when(z < nz - 1)
            def _():
                left(h, z, s).wait_recv()
                acc[h, z, s] += r["lrecv"][h, z, s].astype(F32)

            @pl.when(s != me)
            def _():
                r["xsend"][h, s] = acc[h, z, s].astype(BF16)
                cross(h, s, me).start()

            return carry

        lax.fori_loop(0, n, body, 0)

    def total(h):
        r["sum"][...] = acc[h, z, me]

        def body(p, carry):
            @pl.when(p != me)
            def _():
                cross(h, p, p).wait_recv()
                r["sum"][...] += r["xrecv"][h, p].astype(F32)

            return carry

        lax.fori_loop(0, n, body, 0)
        for p in range(n):
            wg[:, pl.ds((p * heads + h) * HEAD_SIZE, HEAD_SIZE)] = r["sum"][
                :, p * HEAD_SIZE : (p + 1) * HEAD_SIZE
            ] * (1.0 / (2 * nz))

    def drain(h):
        def body(s, carry):
            @pl.when(s != me)
            def _():
                cross(h, s, me).wait_send()

            for c in range(nz):
                @pl.when(z < c)
                def _():
                    right(h, c, s).wait_send()

                @pl.when(z > c)
                def _():
                    left(h, c, s).wait_send()

            return carry

        lax.fori_loop(0, n, body, 0)

    tile = 256
    store = pltpu.make_async_copy(r["outv"], out, loc.at[1])

    def project():
        def body(i, carry):
            at = span(i, tile)
            part = mm(seq[0], wv[0, at, :], 1, 1)
            for h in range(1, heads):
                part += mm(seq[h], wv[h, at, :], 1, 1)
            r["outv"][:, at] = part.astype(BF16)
            return carry

        lax.fori_loop(0, model // tile, body, 0)
        store.start()

    for h in range(heads):
        forward(h)
        cots[h].start()
    for h in range(heads):
        attns[h].arrive()
        give(h)
        take(h)
        burst(h, 0)
        hooks = {n // 2 - 1: lambda: burst(h, 1)}
        if h > 0:
            hooks[0] = lambda: finish(h - 1)
        backward(h, hooks)
        collect(h, {n // 2 - 1: lambda: burst(h, 2)})
        for b in range(3, nz - 1):
            burst(h, b)
    project()
    finish(heads - 1)
    for h in range(heads):
        total(h)
    for h in range(heads):
        drain(h)
    for trade in grads.values():
        trade.arrive()
    for trade in (*rows.values(), *cots, *attns, *grads.values()):
        trade.sent()
    store.wait()


def shards(queries, keys, values, out_weight, out_cot, block_list):
    n = lax.axis_size("ctx")
    n_dp = lax.axis_size("dp")
    nz = n_dp // 2
    _, tokens, total = queries.shape
    model = out_weight.shape[0]
    heads = total // n // HEAD_SIZE
    length = tokens * n
    held = tokens // BLOCK_TOKENS
    blocks, chosen = block_list.shape
    sub = model // (n * n_dp)
    anyspec = pl.BlockSpec(memory_space=pl.ANY)
    vspec = pl.BlockSpec(memory_space=pltpu.VMEM)
    sspec = pl.BlockSpec(memory_space=pltpu.SMEM)
    dma = pltpu.SemaphoreType.DMA

    width = n * HEAD_SIZE
    lane = (heads, nz, n, sub, width)
    cross = (heads, n, sub, width)
    byhead = (heads, length, HEAD_SIZE)
    scratch = {
        "ocv": pltpu.VMEM((tokens, model), BF16),
        "octv": pltpu.VMEM((model, tokens), BF16),
        "wv": pltpu.VMEM((heads, model, width), BF16),
        "seq": pltpu.VMEM((heads, tokens, width), BF16),
        "outv": pltpu.VMEM((tokens, model), BF16),
        "cotbuf": pltpu.VMEM((heads, n, held, BLOCK_TOKENS, HEAD_SIZE), BF16),
        "attn": pltpu.VMEM(byhead, BF16),
        "dq": pltpu.VMEM(byhead, BF16),
        "dk": pltpu.VMEM(byhead, BF16),
        "dv": pltpu.VMEM(byhead, BF16),
        "ps": pltpu.VMEM((heads, blocks * chosen + 1, BLOCK_TOKENS, BLOCK_TOKENS), BF16),
        "dss": pltpu.VMEM((blocks * chosen + 1, BLOCK_TOKENS, BLOCK_TOKENS), BF16),
        "kt": pltpu.VMEM((blocks, HEAD_SIZE, BLOCK_TOKENS), BF16),
        "vt": pltpu.VMEM((blocks, HEAD_SIZE, BLOCK_TOKENS), BF16),
        "acc": pltpu.VMEM(lane, F32),
        "sum": pltpu.VMEM((sub, width), F32),
        "csend": pltpu.VMEM(lane, BF16),
        "crecv": pltpu.VMEM(lane, BF16),
        "zsend": pltpu.VMEM(lane, BF16),
        "rrecv": pltpu.VMEM(lane, BF16),
        "lrecv": pltpu.VMEM(lane, BF16),
        "xsend": pltpu.VMEM(cross, BF16),
        "xrecv": pltpu.VMEM(cross, BF16),
        "pos": pltpu.SMEM((blocks, blocks), jnp.int32),
        "loc": dma((2,)),
        "wsem": dma((heads, n)),
        "in_s": dma((heads, 4, n)),
        "in_r": dma((heads, 4, n)),
        "in_l": dma((heads, 4)),
        "out_s": dma((heads, 4, n)),
        "out_r": dma((heads, 4, n)),
        "out_l": dma((heads, 4)),
        "csem_s": dma((heads, nz)),
        "csem_r": dma((heads, nz)),
        "zsem": dma((heads, nz, n)),
        "rsem": dma((heads, nz, n)),
        "lsem": dma((heads, nz, n)),
        "xsem_s": dma((heads, n)),
        "xsem_r": dma((heads, n)),
    }
    for h in range(heads):
        for t in "qkvc":
            scratch[f"{t}{h}"] = pltpu.VMEM((blocks, BLOCK_TOKENS, HEAD_SIZE), BF16)
    rows = [x.reshape(held, BLOCK_TOKENS, total) for x in (queries, keys, values)]
    bytoken = jax.ShapeDtypeStruct((tokens, total), BF16)
    out, dq, dk, dv, wg = pl.pallas_call(
        functools.partial(layer_kernel, n, nz, heads, tuple(scratch)),
        out_shape=(
            jax.ShapeDtypeStruct((tokens, model), BF16),
            bytoken,
            bytoken,
            bytoken,
            jax.ShapeDtypeStruct((sub, total), F32),
        ),
        in_specs=[sspec] + [anyspec] * 5,
        out_specs=(anyspec, anyspec, anyspec, anyspec, vspec),
        scratch_shapes=list(scratch.values()),
        compiler_params=pltpu.CompilerParams(
            collective_id=0, has_side_effects=True, vmem_limit_bytes=VMEM_BYTES
        ),
    )(block_list.T, *rows, out_weight, out_cot[0])
    return out[None], dq[None], dk[None], dv[None], wg


def solution(mesh):
    part = P("dp", "ctx", None)
    return jax.shard_map(
        shards,
        mesh=mesh,
        in_specs=(part, part, part, P(), part, P()),
        out_specs=(part, part, part, part, P(("dp", "ctx"), None)),
        check_vma=False,
    )
```

```python
import functools
import math

import jax
import jax.numpy as jnp
from jax import lax
from jax.experimental import pallas as pl
from jax.experimental.pallas import tpu as pltpu
from jax.sharding import PartitionSpec as P

HEAD_SIZE = 128
BLOCK_TOKENS = 128
MESH = pl.DeviceIdType.MESH
BF16 = jnp.bfloat16
F32 = jnp.float32
VMEM_BYTES = 52 * 1024 * 1024


def mm(a, b, ca=1, cb=0):
    return lax.dot_general(a, b, (((ca,), (cb,)), ((), ())), preferred_element_type=F32)


def span(i, size):
    return pl.ds(pl.multiple_of(i * size, size), size)


def layer_kernel(n, nz, heads, names, picks, q, k, v, w, oc, out, dqo, dko, dvo, wg, *scratch):
    r = dict(zip(names, scratch))
    me = lax.axis_index("ctx")
    dp = lax.axis_index("dp")
    core = lax.rem(dp, 2)
    other = dp + 1 - 2 * core
    z = dp // 2
    held = q.shape[0]
    tokens = held * BLOCK_TOKENS
    model = w.shape[0]
    chosen, blocks = picks.shape
    sub = wg.shape[0]
    empty = blocks * chosen
    scale = 1.0 / math.sqrt(HEAD_SIZE)
    factor = scale * math.log2(math.e)
    ocv, octv, wv, seq = r["ocv"], r["octv"], r["wv"], r["seq"]
    acc, ps, dss, kt, vt = r["acc"], r["ps"], r["dss"], r["kt"], r["vt"]
    pos, loc = r["pos"], r["loc"]

    barrier = pltpu.get_barrier_semaphore()
    up = lax.rem(z + 1, nz) * 2 + core
    down = lax.rem(z + nz - 1, nz) * 2 + core
    for d in range(1, n):
        pl.semaphore_signal(
            barrier, inc=1, device_id=(dp, lax.rem(me + d, n)), device_id_type=MESH
        )
    for target in (other, up, down):
        pl.semaphore_signal(barrier, inc=1, device_id=(target, me), device_id_type=MESH)
    pl.semaphore_wait(barrier, n - 1 + 3)

    def partner(d):
        return lax.rem(me + d, n)

    def column(p, h):
        return span(p * heads + h, HEAD_SIZE)

    mine = pl.ds(me * held, held)

    class Trade:
        def __init__(self, src_of, dst, sems, where):
            self.src_of, self.dst = src_of, dst
            self.send, self.recv, self.own_sem = (r[sems + x].at[where] for x in "srl")

        def copy(self, d):
            p = partner(d)
            return pltpu.make_async_remote_copy(
                self.src_of(p), self.dst, self.send.at[d], self.recv.at[d],
                device_id=(dp, p), device_id_type=MESH,
            )

        def own(self):
            return pltpu.make_async_copy(self.src_of(me), self.dst, self.own_sem)

        def start(self):
            for d in range(1, n):
                self.copy(d).start()
            self.own().start()

        def arrive(self):
            self.own().wait()
            for d in range(1, n):
                self.copy(d).wait_recv()

        def sent(self):
            for d in range(1, n):
                self.copy(d).wait_send()

    rows = {
        (t, h): Trade(lambda p, x=x, h=h: x.at[:, :, column(p, h)], r[f"{t}{h}"].at[mine], "in_", (h, i))
        for i, (t, x) in enumerate((("k", k), ("q", q), ("v", v)))
        for h in range(heads)
    }
    cots = [
        Trade(lambda p, h=h: r["cotbuf"].at[h, p], r[f"c{h}"].at[mine], "in_", (h, 3))
        for h in range(heads)
    ]
    attns = [
        Trade(
            lambda p, h=h: r["attn"].at[h, span(p, tokens), :],
            seq.at[h, :, span(me, HEAD_SIZE)], "out_", (h, 0),
        )
        for h in range(heads)
    ]
    grads = {
        (t, h): Trade(
            lambda p, h=h, t=t: r[t].at[h, span(p, tokens), :], o.at[:, column(me, h)], "out_", (h, i)
        )
        for i, t, o in ((1, "dq", dqo), (2, "dk", dko), (3, "dv", dvo))
        for h in range(heads)
    }

    for h in range(heads):
        for t in "kqv":
            rows[t, h].start()
    load_oc = pltpu.make_async_copy(oc, ocv, loc.at[0])
    load_oc.start()
    load_w = []
    for h in range(heads):
        for p in range(n):
            copy = pltpu.make_async_copy(
                w.at[:, pl.ds((p * heads + h) * HEAD_SIZE, HEAD_SIZE)],
                wv.at[h, :, pl.ds(p * HEAD_SIZE, HEAD_SIZE)],
                r["wsem"].at[h, p],
            )
            copy.start()
            load_w.append(copy)

    def place(i, carry):
        def one(b, carry):
            at = empty
            for j in range(chosen):
                at = jnp.where(picks[j, i] == b, i * chosen + j, at)
            pos[i, b] = at
            return carry

        return lax.fori_loop(0, blocks, one, carry)

    lax.fori_loop(0, blocks, place, 0)
    for h in range(heads):
        ps[h, empty] = jnp.zeros((BLOCK_TOKENS, BLOCK_TOKENS), BF16)
    dss[empty] = jnp.zeros((BLOCK_TOKENS, BLOCK_TOKENS), BF16)

    load_oc.wait()

    def flip(i, carry):
        octv[span(i, 256), :] = ocv[:, span(i, 256)].T
        return carry

    lax.fori_loop(0, model // 256, flip, 0)
    for copy in load_w:
        copy.wait()

    def work_cot(h):
        def body(p, carry):
            r["cotbuf"][h, p] = (
                mm(ocv[...], wv[h, :, span(p, HEAD_SIZE)])
                .astype(BF16)
                .reshape(held, BLOCK_TOKENS, HEAD_SIZE)
            )
            return carry

        lax.fori_loop(0, n, body, 0)

    for h in range(heads):
        work_cot(h)

    def listed(ref, i, axis):
        return jnp.concatenate([ref[picks[j, i]] for j in range(chosen)], axis=axis)

    def forward_block(h, i):
        st = mm(listed(r[f"k{h}"], i, 0), r[f"q{h}"][i], 1, 1)
        top = jnp.max(st, axis=0, keepdims=True)
        e = jnp.exp2((st - top) * factor)
        inv = 1.0 / jnp.sum(e, axis=0, keepdims=True)
        low = (e * inv).astype(BF16)
        a = mm(listed(vt, i, 1), low).astype(BF16)
        r["attn"][h, span(i, BLOCK_TOKENS), :] = a.T
        for j in range(chosen):
            ps[h, i * chosen + j] = low[j * BLOCK_TOKENS : (j + 1) * BLOCK_TOKENS]

    def backward_block(h, i):
        at = span(i, BLOCK_TOKENS)
        ci = r[f"c{h}"][i]
        dpt = mm(listed(r[f"v{h}"], i, 0), ci, 1, 1)
        dot = jnp.sum(
            (ci.astype(F32) * r["attn"][h, at, :].astype(F32)).T, axis=0, keepdims=True
        )
        parts = []
        for j in range(chosen):
            part = slice(j * BLOCK_TOKENS, (j + 1) * BLOCK_TOKENS)
            ds = (ps[h, i * chosen + j].astype(F32) * (dpt[part] - dot)).astype(BF16)
            dss[i * chosen + j] = ds
            parts.append(ds)
        r["dq"][h, at, :] = (mm(listed(kt, i, 1), jnp.concatenate(parts, axis=0)) * scale).T.astype(BF16)

    def collect_part(h, p):
        def wide(kept):
            return jnp.concatenate(
                [
                    jnp.concatenate([kept(pos[i, p * held + x]) for i in range(blocks)], axis=1)
                    for x in range(held)
                ],
                axis=0,
            )

        at = span(p, tokens)
        pst = wide(lambda slot: ps[h, slot])
        r["dv"][h, at, :] = mm(pst, r[f"c{h}"][...].reshape(-1, HEAD_SIZE)).astype(BF16)
        dst = wide(lambda slot: dss[slot])
        r["dk"][h, at, :] = (mm(dst, r[f"q{h}"][...].reshape(-1, HEAD_SIZE)) * scale).astype(BF16)

    def turn(src, dst):
        def body(b, carry):
            dst[b] = src[b].T
            return carry

        lax.fori_loop(0, blocks, body, 0)

    def by_partner(work, trades, hooks):
        def body(t, carry):
            d = t + 1
            work(partner(d))

            @pl.when(d < n)
            def _():
                for trade in trades:
                    trade.copy(d).start()

            for at, hook in hooks.items():
                pl.when(t == at)(hook)
            return carry

        lax.fori_loop(0, n, body, 0)
        for trade in trades:
            trade.own().start()

    def forward(h):
        for t in "kqv":
            rows[t, h].arrive()
        turn(r[f"v{h}"], vt)

        def work(p):
            for x in range(held):
                forward_block(h, p * held + x)

        by_partner(work, [attns[h]], {})

    def backward(h, hooks):
        turn(r[f"k{h}"], kt)
        cots[h].arrive()

        def work(p):
            for x in range(held):
                backward_block(h, p * held + x)

        by_partner(work, [grads["dq", h]], hooks)

    def collect(h, hooks):
        by_partner(lambda p: collect_part(h, p), [grads["dv", h], grads["dk", h]], hooks)

    def term(h, c, who):
        return mm(octv[span(2 * c + who, n * sub), :], seq[h]).reshape(n, sub, -1)

    def core_copy(h, c):
        return pltpu.make_async_remote_copy(
            r["csend"].at[h, c], r["crecv"].at[h, c], r["csem_s"].at[h, c], r["csem_r"].at[h, c],
            device_id=(other, me), device_id_type=MESH,
        )

    def give(h):
        def body(c, carry):
            r["csend"][h, c] = term(h, c, 1 - core).astype(BF16)
            core_copy(h, c).start()
            return carry

        lax.fori_loop(0, nz, body, 0)

        def keep(c, carry):
            acc[h, c] = term(h, c, core)
            return carry

        lax.fori_loop(0, nz, keep, 0)

    def take(h):
        def body(c, carry):
            core_copy(h, c).wait()
            for s in range(n):
                acc[h, c, s] += r["crecv"][h, c, s].astype(F32)
            return carry

        lax.fori_loop(0, nz, body, 0)

    def hop(h, c, s, buf, sem, target):
        return pltpu.make_async_remote_copy(
            r["zsend"].at[h, c, s], r[buf].at[h, c, s], r["zsem"].at[h, c, s],
            r[sem].at[h, c, s], device_id=(target, me), device_id_type=MESH,
        )

    def right(h, c, s):
        return hop(h, c, s, "rrecv", "rsem", up)

    def left(h, c, s):
        return hop(h, c, s, "lrecv", "lsem", down)

    def burst(h, b):
        def one_way(rank, chunk_of, link, buf):
            count = jnp.where(rank == 0, nz - 1 if b == 0 else 0, jnp.where(rank <= b, 1, 0))

            def body(i, carry):
                c = chunk_of(b - rank + i // n)
                s = lax.rem(i, n)

                @pl.when(rank > 0)
                def _():
                    link(h, c, s).wait_recv()
                    acc[h, c, s] += r[buf][h, c, s].astype(F32)

                r["zsend"][h, c, s] = acc[h, c, s].astype(BF16)
                link(h, c, s).start()
                return carry

            lax.fori_loop(0, count * n, body, 0)

        one_way(z, lambda x: nz - 1 - x, right, "rrecv")
        one_way(nz - 1 - z, lambda x: x, left, "lrecv")

    def cross(h, s, slot):
        return pltpu.make_async_remote_copy(
            r["xsend"].at[h, s], r["xrecv"].at[h, slot], r["xsem_s"].at[h, s],
            r["xsem_r"].at[h, slot], device_id=(dp, s), device_id_type=MESH,
        )

    def finish(h):
        def body(s, carry):
            @pl.when(z > 0)
            def _():
                right(h, z, s).wait_recv()
                acc[h, z, s] += r["rrecv"][h, z, s].astype(F32)

            @pl.when(z < nz - 1)
            def _():
                left(h, z, s).wait_recv()
                acc[h, z, s] += r["lrecv"][h, z, s].astype(F32)

            @pl.when(s != me)
            def _():
                r["xsend"][h, s] = acc[h, z, s].astype(BF16)
                cross(h, s, me).start()

            return carry

        lax.fori_loop(0, n, body, 0)

    def total(h):
        r["sum"][...] = acc[h, z, me]

        def body(p, carry):
            @pl.when(p != me)
            def _():
                cross(h, p, p).wait_recv()
                r["sum"][...] += r["xrecv"][h, p].astype(F32)

            return carry

        lax.fori_loop(0, n, body, 0)
        for p in range(n):
            wg[:, pl.ds((p * heads + h) * HEAD_SIZE, HEAD_SIZE)] = r["sum"][
                :, p * HEAD_SIZE : (p + 1) * HEAD_SIZE
            ] * (1.0 / (2 * nz))

    def drain(h):
        def body(s, carry):
            @pl.when(s != me)
            def _():
                cross(h, s, me).wait_send()

            for c in range(nz):
                @pl.when(z < c)
                def _():
                    right(h, c, s).wait_send()

                @pl.when(z > c)
                def _():
                    left(h, c, s).wait_send()

            return carry

        lax.fori_loop(0, n, body, 0)

    tile = 256

    def project():
        def body(i, carry):
            at = span(i, tile)
            part = mm(seq[0], wv[0, at, :], 1, 1)
            for h in range(1, heads):
                part += mm(seq[h], wv[h, at, :], 1, 1)
            out[:, at] = part.astype(BF16)
            return carry

        lax.fori_loop(0, model // tile, body, 0)

    for h in range(heads):
        forward(h)
        cots[h].start()
    for h in range(heads):
        attns[h].arrive()
        give(h)
        take(h)
        burst(h, 0)
        hooks = {n // 2 - 1: lambda: burst(h, 1)}
        if h > 0:
            hooks[0] = lambda: finish(h - 1)
        backward(h, hooks)
        collect(h, {n // 2 - 1: lambda: burst(h, 2)})
        for b in range(3, nz - 1):
            burst(h, b)
    project()
    finish(heads - 1)
    for h in range(heads):
        total(h)
    for h in range(heads):
        drain(h)
    for trade in grads.values():
        trade.arrive()
    for trade in (*rows.values(), *cots, *attns, *grads.values()):
        trade.sent()


def store_kernel(*refs):
    sems = refs[-1]
    copies = [
        pltpu.make_async_copy(refs[i], refs[5 + i], sems.at[i]) for i in range(5)
    ]
    for copy in copies:
        copy.start()
    for copy in copies:
        copy.wait()


def shards(queries, keys, values, out_weight, out_cot, block_list):
    n = lax.axis_size("ctx")
    n_dp = lax.axis_size("dp")
    nz = n_dp // 2
    _, tokens, total = queries.shape
    model = out_weight.shape[0]
    heads = total // n // HEAD_SIZE
    length = tokens * n
    held = tokens // BLOCK_TOKENS
    blocks, chosen = block_list.shape
    sub = model // (n * n_dp)
    anyspec = pl.BlockSpec(memory_space=pl.ANY)
    vspec = pl.BlockSpec(memory_space=pltpu.VMEM)
    sspec = pl.BlockSpec(memory_space=pltpu.SMEM)
    dma = pltpu.SemaphoreType.DMA

    width = n * HEAD_SIZE
    lane = (heads, nz, n, sub, width)
    cross = (heads, n, sub, width)
    byhead = (heads, length, HEAD_SIZE)
    scratch = {
        "ocv": pltpu.VMEM((tokens, model), BF16),
        "octv": pltpu.VMEM((model, tokens), BF16),
        "wv": pltpu.VMEM((heads, model, width), BF16),
        "seq": pltpu.VMEM((heads, tokens, width), BF16),
        "cotbuf": pltpu.VMEM((heads, n, held, BLOCK_TOKENS, HEAD_SIZE), BF16),
        "attn": pltpu.VMEM(byhead, BF16),
        "dq": pltpu.VMEM(byhead, BF16),
        "dk": pltpu.VMEM(byhead, BF16),
        "dv": pltpu.VMEM(byhead, BF16),
        "ps": pltpu.VMEM((heads, blocks * chosen + 1, BLOCK_TOKENS, BLOCK_TOKENS), BF16),
        "dss": pltpu.VMEM((blocks * chosen + 1, BLOCK_TOKENS, BLOCK_TOKENS), BF16),
        "kt": pltpu.VMEM((blocks, HEAD_SIZE, BLOCK_TOKENS), BF16),
        "vt": pltpu.VMEM((blocks, HEAD_SIZE, BLOCK_TOKENS), BF16),
        "acc": pltpu.VMEM(lane, F32),
        "sum": pltpu.VMEM((sub, width), F32),
        "csend": pltpu.VMEM(lane, BF16),
        "crecv": pltpu.VMEM(lane, BF16),
        "zsend": pltpu.VMEM(lane, BF16),
        "rrecv": pltpu.VMEM(lane, BF16),
        "lrecv": pltpu.VMEM(lane, BF16),
        "xsend": pltpu.VMEM(cross, BF16),
        "xrecv": pltpu.VMEM(cross, BF16),
        "pos": pltpu.SMEM((blocks, blocks), jnp.int32),
        "loc": dma((1,)),
        "wsem": dma((heads, n)),
        "in_s": dma((heads, 4, n)),
        "in_r": dma((heads, 4, n)),
        "in_l": dma((heads, 4)),
        "out_s": dma((heads, 4, n)),
        "out_r": dma((heads, 4, n)),
        "out_l": dma((heads, 4)),
        "csem_s": dma((heads, nz)),
        "csem_r": dma((heads, nz)),
        "zsem": dma((heads, nz, n)),
        "rsem": dma((heads, nz, n)),
        "lsem": dma((heads, nz, n)),
        "xsem_s": dma((heads, n)),
        "xsem_r": dma((heads, n)),
    }
    for h in range(heads):
        for t in "qkvc":
            scratch[f"{t}{h}"] = pltpu.VMEM((blocks, BLOCK_TOKENS, HEAD_SIZE), BF16)
    rows = [x.reshape(held, BLOCK_TOKENS, total) for x in (queries, keys, values)]
    bytoken = jax.ShapeDtypeStruct((tokens, total), BF16)
    results = (
        jax.ShapeDtypeStruct((tokens, model), BF16),
        bytoken,
        bytoken,
        bytoken,
        jax.ShapeDtypeStruct((sub, total), F32),
    )
    held_results = pl.pallas_call(
        functools.partial(layer_kernel, n, nz, heads, tuple(scratch)),
        out_shape=tuple(pltpu.VMEM(x.shape, x.dtype) for x in results),
        in_specs=[sspec] + [anyspec] * 5,
        out_specs=(vspec,) * 5,
        scratch_shapes=list(scratch.values()),
        compiler_params=pltpu.CompilerParams(
            collective_id=0, has_side_effects=True, vmem_limit_bytes=VMEM_BYTES
        ),
    )(block_list.T, *rows, out_weight, out_cot[0])
    out, dq, dk, dv, wg = pl.pallas_call(
        store_kernel,
        out_shape=results,
        in_specs=[vspec] * 5,
        out_specs=(anyspec,) * 5,
        scratch_shapes=[dma((5,))], compiler_params=pltpu.CompilerParams(vmem_limit_bytes=1024 * 1024),
    )(*[pltpu.with_memory_space_constraint(x, pltpu.VMEM) for x in held_results])
    return out[None], dq[None], dk[None], dv[None], wg


def solution(mesh):
    part = P("dp", "ctx", None)
    return jax.shard_map(
        shards,
        mesh=mesh,
        in_specs=(part, part, part, P(), part, P()),
        out_specs=(part, part, part, part, P(("dp", "ctx"), None)),
        check_vma=False,
    )
```

```python
import functools
import math

import jax
import jax.numpy as jnp
from jax import lax
from jax.experimental import pallas as pl
from jax.experimental.pallas import tpu as pltpu
from jax.sharding import PartitionSpec as P

HEAD_SIZE = 128
BLOCK_TOKENS = 128
EARLY = 2
MESH = pl.DeviceIdType.MESH
BF16 = jnp.bfloat16
F32 = jnp.float32
VMEM_BYTES = 52 * 1024 * 1024


def mm(a, b, ca=1, cb=0):
    return lax.dot_general(a, b, (((ca,), (cb,)), ((), ())), preferred_element_type=F32)


def span(i, size):
    return pl.ds(pl.multiple_of(i * size, size), size)


def layer_kernel(n, nz, heads, names, picks, q, k, v, w, oc, out, dqo, dko, dvo, wg, *scratch):
    r = dict(zip(names, scratch))
    me = lax.axis_index("ctx")
    dp = lax.axis_index("dp")
    core = lax.rem(dp, 2)
    other = dp + 1 - 2 * core
    z = dp // 2
    held = q.shape[0]
    tokens = held * BLOCK_TOKENS
    model = w.shape[0]
    chosen, blocks = picks.shape
    sub = wg.shape[0]
    empty = blocks * chosen
    scale = 1.0 / math.sqrt(HEAD_SIZE)
    factor = scale * math.log2(math.e)
    ocv, octv, wv, seq = r["ocv"], r["octv"], r["wv"], r["seq"]
    acc, ps, dss, kt, vt = r["acc"], r["ps"], r["dss"], r["kt"], r["vt"]
    pos, loc = r["pos"], r["loc"]

    barrier = pltpu.get_barrier_semaphore()
    up = lax.rem(z + 1, nz) * 2 + core
    down = lax.rem(z + nz - 1, nz) * 2 + core
    for d in range(1, n):
        pl.semaphore_signal(
            barrier, inc=1, device_id=(dp, lax.rem(me + d, n)), device_id_type=MESH
        )
    pl.semaphore_signal(barrier, inc=1, device_id=(other, me), device_id_type=MESH)

    @pl.when(z < nz - 1)
    def _():
        pl.semaphore_signal(barrier, inc=1, device_id=(up, me), device_id_type=MESH)

    @pl.when(z > 0)
    def _():
        pl.semaphore_signal(barrier, inc=1, device_id=(down, me), device_id_type=MESH)

    ends = jnp.where(z == 0, 1, 0) + jnp.where(z == nz - 1, 1, 0)
    pl.semaphore_wait(barrier, n - 1 + 3 - ends)

    def partner(d):
        return lax.rem(me + d, n)

    def column(p, h):
        return span(p * heads + h, HEAD_SIZE)

    mine = pl.ds(me * held, held)

    class Trade:
        def __init__(self, src_of, dst, sems, where):
            self.src_of, self.dst = src_of, dst
            self.send, self.recv, self.own_sem = (r[sems + x].at[where] for x in "srl")

        def copy(self, d):
            p = partner(d)
            return pltpu.make_async_remote_copy(
                self.src_of(p), self.dst, self.send.at[d], self.recv.at[d],
                device_id=(dp, p), device_id_type=MESH,
            )

        def own(self):
            return pltpu.make_async_copy(self.src_of(me), self.dst, self.own_sem)

        def start(self):
            for d in range(1, n):
                self.copy(d).start()
            self.own().start()

        def arrive(self):
            self.own().wait()
            for d in range(1, n):
                self.copy(d).wait_recv()

        def sent(self):
            for d in range(1, n):
                self.copy(d).wait_send()

    rows = {
        (t, h): Trade(lambda p, x=x, h=h: x.at[:, :, column(p, h)], r[f"{t}{h}"].at[mine], "in_", (h, i))
        for i, (t, x) in enumerate((("k", k), ("q", q), ("v", v)))
        for h in range(heads)
    }
    cots = [
        Trade(lambda p, h=h: r["cotbuf"].at[h, p], r[f"c{h}"].at[mine], "in_", (h, 3))
        for h in range(heads)
    ]
    attns = [
        Trade(
            lambda p, h=h: r["attn"].at[h, span(p, tokens), :],
            seq.at[h, :, span(me, HEAD_SIZE)], "out_", (h, 0),
        )
        for h in range(heads)
    ]
    grads = {
        (t, h): Trade(
            lambda p, h=h, t=t: r[t].at[h, span(p, tokens), :], o.at[:, column(me, h)], "out_", (h, i)
        )
        for i, t, o in ((1, "dq", dqo), (2, "dk", dko), (3, "dv", dvo))
        for h in range(heads)
    }

    order = [rows[t, h] for h in range(heads) for t in "kqv"]

    def send_rows(first, last):
        for trade in order[first:last]:
            trade.start()

    send_rows(0, 3 + EARLY)
    load_oc = pltpu.make_async_copy(oc, ocv, loc.at[0])
    load_oc.start()
    load_w = []
    for h in range(heads):
        for p in range(n):
            copy = pltpu.make_async_copy(
                w.at[:, pl.ds((p * heads + h) * HEAD_SIZE, HEAD_SIZE)],
                wv.at[h, :, pl.ds(p * HEAD_SIZE, HEAD_SIZE)],
                r["wsem"].at[h, p],
            )
            copy.start()
            load_w.append(copy)

    def place(i, carry):
        def one(b, carry):
            at = empty
            for j in range(chosen):
                at = jnp.where(picks[j, i] == b, i * chosen + j, at)
            pos[i, b] = at
            return carry

        return lax.fori_loop(0, blocks, one, carry)

    lax.fori_loop(0, blocks, place, 0)
    for h in range(heads):
        ps[h, empty] = jnp.zeros((BLOCK_TOKENS, BLOCK_TOKENS), BF16)
    dss[empty] = jnp.zeros((BLOCK_TOKENS, BLOCK_TOKENS), BF16)

    load_oc.wait()

    def flip(i, carry):
        octv[span(i, 256), :] = ocv[:, span(i, 256)].T
        return carry

    lax.fori_loop(0, model // 256, flip, 0)
    for copy in load_w:
        copy.wait()

    def work_cot(h):
        def body(p, carry):
            r["cotbuf"][h, p] = (
                mm(ocv[...], wv[h, :, span(p, HEAD_SIZE)])
                .astype(BF16)
                .reshape(held, BLOCK_TOKENS, HEAD_SIZE)
            )
            return carry

        lax.fori_loop(0, n, body, 0)

    for h in range(heads):
        work_cot(h)

    def listed(ref, i, axis):
        return jnp.concatenate([ref[picks[j, i]] for j in range(chosen)], axis=axis)

    def score_block(h, i):
        st = mm(listed(r[f"k{h}"], i, 0), r[f"q{h}"][i], 1, 1)
        top = jnp.max(st, axis=0, keepdims=True)
        e = jnp.exp2((st - top) * factor)
        inv = 1.0 / jnp.sum(e, axis=0, keepdims=True)
        low = (e * inv).astype(BF16)
        ps[h, pl.ds(i * chosen, chosen)] = low.reshape(chosen, BLOCK_TOKENS, BLOCK_TOKENS)

    def mix_block(h, i):
        low = ps[h, pl.ds(i * chosen, chosen)].reshape(-1, BLOCK_TOKENS)
        a = mm(listed(vt, i, 1), low).astype(BF16)
        r["attn"][h, span(i, BLOCK_TOKENS), :] = a.T

    def backward_block(h, i):
        at = span(i, BLOCK_TOKENS)
        ci = r[f"c{h}"][i]
        dpt = mm(listed(r[f"v{h}"], i, 0), ci, 1, 1)
        dot = jnp.sum(
            (ci.astype(F32) * r["attn"][h, at, :].astype(F32)).T, axis=0, keepdims=True
        )
        parts = []
        for j in range(chosen):
            part = slice(j * BLOCK_TOKENS, (j + 1) * BLOCK_TOKENS)
            ds = (ps[h, i * chosen + j].astype(F32) * (dpt[part] - dot)).astype(BF16)
            dss[i * chosen + j] = ds
            parts.append(ds)
        r["dq"][h, at, :] = (mm(listed(kt, i, 1), jnp.concatenate(parts, axis=0)) * scale).T.astype(BF16)

    def collect_part(h, p):
        def wide(kept):
            return jnp.concatenate(
                [
                    jnp.concatenate([kept(pos[i, p * held + x]) for i in range(blocks)], axis=1)
                    for x in range(held)
                ],
                axis=0,
            )

        at = span(p, tokens)
        pst = wide(lambda slot: ps[h, slot])
        r["dv"][h, at, :] = mm(pst, r[f"c{h}"][...].reshape(-1, HEAD_SIZE)).astype(BF16)
        dst = wide(lambda slot: dss[slot])
        r["dk"][h, at, :] = (mm(dst, r[f"q{h}"][...].reshape(-1, HEAD_SIZE)) * scale).astype(BF16)

    def turn(src, dst):
        def body(b, carry):
            dst[b] = src[b].T
            return carry

        lax.fori_loop(0, blocks, body, 0)

    def by_partner(work, trades, hooks):
        def body(t, carry):
            d = t + 1
            work(partner(d))

            @pl.when(d < n)
            def _():
                for trade in trades:
                    trade.copy(d).start()

            for at, hook in hooks.items():
                pl.when(t == at)(hook)
            return carry

        lax.fori_loop(0, n, body, 0)
        for trade in trades:
            trade.own().start()

    def score(h):
        for t in "kq":
            rows[t, h].arrive()

        def body(p, carry):
            for x in range(held):
                score_block(h, p * held + x)
            return carry

        lax.fori_loop(0, n, body, 0)

    def mix(h):
        rows["v", h].arrive()
        turn(r[f"v{h}"], vt)

        def work(p):
            for x in range(held):
                mix_block(h, p * held + x)

        by_partner(work, [attns[h]], {})

    def backward(h, hooks):
        turn(r[f"k{h}"], kt)
        cots[h].arrive()

        def work(p):
            for x in range(held):
                backward_block(h, p * held + x)

        by_partner(work, [grads["dq", h]], hooks)

    def collect(h, hooks):
        by_partner(lambda p: collect_part(h, p), [grads["dv", h], grads["dk", h]], hooks)

    def term(h, c, who):
        return mm(octv[span(2 * c + who, n * sub), :], seq[h]).reshape(n, sub, -1)

    def core_copy(h, c):
        return pltpu.make_async_remote_copy(
            r["csend"].at[h, c], r["crecv"].at[h, c], r["csem_s"].at[h, c], r["csem_r"].at[h, c],
            device_id=(other, me), device_id_type=MESH,
        )

    def give(h):
        def body(c, carry):
            r["csend"][h, c] = term(h, c, 1 - core).astype(BF16)
            core_copy(h, c).start()
            return carry

        lax.fori_loop(0, nz, body, 0)

        def keep(c, carry):
            acc[h, c] = term(h, c, core)
            return carry

        lax.fori_loop(0, nz, keep, 0)

    def take(h):
        def body(c, carry):
            core_copy(h, c).wait()
            for s in range(n):
                acc[h, c, s] += r["crecv"][h, c, s].astype(F32)
            return carry

        lax.fori_loop(0, nz, body, 0)

    def hop(h, c, s, buf, sem, target):
        return pltpu.make_async_remote_copy(
            r["zsend"].at[h, c, s], r[buf].at[h, c, s], r["zsem"].at[h, c, s],
            r[sem].at[h, c, s], device_id=(target, me), device_id_type=MESH,
        )

    def right(h, c, s):
        return hop(h, c, s, "rrecv", "rsem", up)

    def left(h, c, s):
        return hop(h, c, s, "lrecv", "lsem", down)

    def burst(h, b):
        def one_way(rank, chunk_of, link, buf):
            count = jnp.where(rank == 0, nz - 1 if b == 0 else 0, jnp.where(rank <= b, 1, 0))

            def body(i, carry):
                c = chunk_of(b - rank + i // n)
                s = lax.rem(i, n)

                @pl.when(rank > 0)
                def _():
                    link(h, c, s).wait_recv()
                    acc[h, c, s] += r[buf][h, c, s].astype(F32)

                r["zsend"][h, c, s] = acc[h, c, s].astype(BF16)
                link(h, c, s).start()
                return carry

            lax.fori_loop(0, count * n, body, 0)

        one_way(z, lambda x: nz - 1 - x, right, "rrecv")
        one_way(nz - 1 - z, lambda x: x, left, "lrecv")

    def cross(h, s, slot):
        return pltpu.make_async_remote_copy(
            r["xsend"].at[h, s], r["xrecv"].at[h, slot], r["xsem_s"].at[h, s],
            r["xsem_r"].at[h, slot], device_id=(dp, s), device_id_type=MESH,
        )

    def finish(h):
        def body(s, carry):
            @pl.when(z > 0)
            def _():
                right(h, z, s).wait_recv()
                acc[h, z, s] += r["rrecv"][h, z, s].astype(F32)

            @pl.when(z < nz - 1)
            def _():
                left(h, z, s).wait_recv()
                acc[h, z, s] += r["lrecv"][h, z, s].astype(F32)

            @pl.when(s != me)
            def _():
                r["xsend"][h, s] = acc[h, z, s].astype(BF16)
                cross(h, s, me).start()

            return carry

        lax.fori_loop(0, n, body, 0)

    def total(h):
        r["sum"][...] = acc[h, z, me]

        def body(p, carry):
            @pl.when(p != me)
            def _():
                cross(h, p, p).wait_recv()
                r["sum"][...] += r["xrecv"][h, p].astype(F32)

            return carry

        lax.fori_loop(0, n, body, 0)
        for p in range(n):
            wg[:, pl.ds((p * heads + h) * HEAD_SIZE, HEAD_SIZE)] = r["sum"][
                :, p * HEAD_SIZE : (p + 1) * HEAD_SIZE
            ] * (1.0 / (2 * nz))

    def drain(h):
        def body(s, carry):
            @pl.when(s != me)
            def _():
                cross(h, s, me).wait_send()

            for c in range(nz):
                @pl.when(z < c)
                def _():
                    right(h, c, s).wait_send()

                @pl.when(z > c)
                def _():
                    left(h, c, s).wait_send()

            return carry

        lax.fori_loop(0, n, body, 0)

    tile = 256

    def project():
        def body(i, carry):
            at = span(i, tile)
            part = mm(seq[0], wv[0, at, :], 1, 1)
            for h in range(1, heads):
                part += mm(seq[h], wv[h, at, :], 1, 1)
            out[:, at] = part.astype(BF16)
            return carry

        lax.fori_loop(0, model // tile, body, 0)

    def begin(h):
        take(h)
        burst(h, 0)

    half = n // 2 - 1
    last = n - 1
    score(0)
    mix(0)
    send_rows(3 + EARLY, 6 + EARLY)
    for h in range(1, heads):
        score(h)
        attns[h - 1].arrive()
        give(h - 1)
        cots[h - 1].start()
        mix(h)
        send_rows(3 * h + 3 + EARLY, 3 * h + 6 + EARLY)
        begin(h - 1)
    cots[heads - 1].start()
    for h in range(heads):
        if h == heads - 1:
            attns[h].arrive()
            give(h)
        if h == 0 and heads > 1:
            backward(h, {half: lambda: burst(h, 1)})
            burst(h, 2)
        elif h == heads - 1:
            hooks = {half: lambda: begin(h)}
            if h > 0:
                hooks[0] = lambda: finish(h - 1)
            backward(h, hooks)
            burst(h, 1)
        else:
            backward(h, {half: lambda: finish(h - 1), last: lambda: burst(h, 1)})
            burst(h, 2)
        if h == heads - 1:
            collect(h, {half: lambda: burst(h, 2)})
        else:
            collect(h, {})
        for b in range(3, nz - 1):
            burst(h, b)
    project()
    finish(heads - 1)
    for h in range(heads):
        total(h)
    for h in range(heads):
        drain(h)
    for trade in grads.values():
        trade.arrive()
    for trade in (*rows.values(), *cots, *attns, *grads.values()):
        trade.sent()


def store_kernel(*refs):
    sems = refs[-1]
    copies = [
        pltpu.make_async_copy(refs[i], refs[5 + i], sems.at[i]) for i in range(5)
    ]
    for copy in copies:
        copy.start()
    for copy in copies:
        copy.wait()


def shards(queries, keys, values, out_weight, out_cot, block_list):
    n = lax.axis_size("ctx")
    n_dp = lax.axis_size("dp")
    nz = n_dp // 2
    _, tokens, total = queries.shape
    model = out_weight.shape[0]
    heads = total // n // HEAD_SIZE
    length = tokens * n
    held = tokens // BLOCK_TOKENS
    blocks, chosen = block_list.shape
    sub = model // (n * n_dp)
    anyspec = pl.BlockSpec(memory_space=pl.ANY)
    vspec = pl.BlockSpec(memory_space=pltpu.VMEM)
    sspec = pl.BlockSpec(memory_space=pltpu.SMEM)
    dma = pltpu.SemaphoreType.DMA

    width = n * HEAD_SIZE
    lane = (heads, nz, n, sub, width)
    cross = (heads, n, sub, width)
    byhead = (heads, length, HEAD_SIZE)
    scratch = {
        "ocv": pltpu.VMEM((tokens, model), BF16),
        "octv": pltpu.VMEM((model, tokens), BF16),
        "wv": pltpu.VMEM((heads, model, width), BF16),
        "seq": pltpu.VMEM((heads, tokens, width), BF16),
        "cotbuf": pltpu.VMEM((heads, n, held, BLOCK_TOKENS, HEAD_SIZE), BF16),
        "attn": pltpu.VMEM(byhead, BF16),
        "dq": pltpu.VMEM(byhead, BF16),
        "dk": pltpu.VMEM(byhead, BF16),
        "dv": pltpu.VMEM(byhead, BF16),
        "ps": pltpu.VMEM((heads, blocks * chosen + 1, BLOCK_TOKENS, BLOCK_TOKENS), BF16),
        "dss": pltpu.VMEM((blocks * chosen + 1, BLOCK_TOKENS, BLOCK_TOKENS), BF16),
        "kt": pltpu.VMEM((blocks, HEAD_SIZE, BLOCK_TOKENS), BF16),
        "vt": pltpu.VMEM((blocks, HEAD_SIZE, BLOCK_TOKENS), BF16),
        "acc": pltpu.VMEM(lane, F32),
        "sum": pltpu.VMEM((sub, width), F32),
        "csend": pltpu.VMEM(lane, BF16),
        "crecv": pltpu.VMEM(lane, BF16),
        "zsend": pltpu.VMEM(lane, BF16),
        "rrecv": pltpu.VMEM(lane, BF16),
        "lrecv": pltpu.VMEM(lane, BF16),
        "xsend": pltpu.VMEM(cross, BF16),
        "xrecv": pltpu.VMEM(cross, BF16),
        "pos": pltpu.SMEM((blocks, blocks), jnp.int32),
        "loc": dma((1,)),
        "wsem": dma((heads, n)),
        "in_s": dma((heads, 4, n)),
        "in_r": dma((heads, 4, n)),
        "in_l": dma((heads, 4)),
        "out_s": dma((heads, 4, n)),
        "out_r": dma((heads, 4, n)),
        "out_l": dma((heads, 4)),
        "csem_s": dma((heads, nz)),
        "csem_r": dma((heads, nz)),
        "zsem": dma((heads, nz, n)),
        "rsem": dma((heads, nz, n)),
        "lsem": dma((heads, nz, n)),
        "xsem_s": dma((heads, n)),
        "xsem_r": dma((heads, n)),
    }
    for h in range(heads):
        for t in "qkvc":
            scratch[f"{t}{h}"] = pltpu.VMEM((blocks, BLOCK_TOKENS, HEAD_SIZE), BF16)
    rows = [x.reshape(held, BLOCK_TOKENS, total) for x in (queries, keys, values)]
    bytoken = jax.ShapeDtypeStruct((tokens, total), BF16)
    results = (
        jax.ShapeDtypeStruct((tokens, model), BF16),
        bytoken,
        bytoken,
        bytoken,
        jax.ShapeDtypeStruct((sub, total), F32),
    )
    held_results = pl.pallas_call(
        functools.partial(layer_kernel, n, nz, heads, tuple(scratch)),
        out_shape=tuple(pltpu.VMEM(x.shape, x.dtype) for x in results),
        in_specs=[sspec] + [anyspec] * 5,
        out_specs=(vspec,) * 5,
        scratch_shapes=list(scratch.values()),
        compiler_params=pltpu.CompilerParams(
            collective_id=0, has_side_effects=True, vmem_limit_bytes=VMEM_BYTES
        ),
    )(block_list.T, *rows, out_weight, out_cot[0])
    out, dq, dk, dv, wg = pl.pallas_call(
        store_kernel,
        out_shape=results,
        in_specs=[vspec] * 5,
        out_specs=(anyspec,) * 5,
        scratch_shapes=[dma((5,))], compiler_params=pltpu.CompilerParams(vmem_limit_bytes=1024 * 1024),
    )(*[pltpu.with_memory_space_constraint(x, pltpu.VMEM) for x in held_results])
    return out[None], dq[None], dk[None], dv[None], wg


def solution(mesh):
    part = P("dp", "ctx", None)
    return jax.shard_map(
        shards,
        mesh=mesh,
        in_specs=(part, part, part, P(), part, P()),
        out_specs=(part, part, part, part, P(("dp", "ctx"), None)),
        check_vma=False,
    )
```

```python
import functools
import math

import jax
import jax.numpy as jnp
from jax import lax
from jax.experimental import pallas as pl
from jax.experimental.pallas import tpu as pltpu
from jax.sharding import PartitionSpec as P

HEAD_SIZE = 128
BLOCK_TOKENS = 128
EARLY = 2
MESH = pl.DeviceIdType.MESH
BF16 = jnp.bfloat16
F32 = jnp.float32
VMEM_BYTES = 52 * 1024 * 1024


def mm(a, b, ca=1, cb=0):
    return lax.dot_general(a, b, (((ca,), (cb,)), ((), ())), preferred_element_type=F32)


def span(i, size):
    return pl.ds(pl.multiple_of(i * size, size), size)


def layer_kernel(n, nz, heads, names, picks, q, k, v, w, oc, out, dqo, dko, dvo, wg, *scratch):
    r = dict(zip(names, scratch))
    me = lax.axis_index("ctx")
    dp = lax.axis_index("dp")
    core = lax.rem(dp, 2)
    other = dp + 1 - 2 * core
    z = dp // 2
    held = q.shape[0]
    tokens = held * BLOCK_TOKENS
    model = w.shape[0]
    chosen, blocks = picks.shape
    sub = wg.shape[0]
    empty = blocks * chosen
    scale = 1.0 / math.sqrt(HEAD_SIZE)
    factor = scale * math.log2(math.e)
    ocv, octv, wv, seq = r["ocv"], r["octv"], r["wv"], r["seq"]
    acc, ps, dss, kt, vt = r["acc"], r["ps"], r["dss"], r["kt"], r["vt"]
    pos, loc = r["pos"], r["loc"]

    barrier = pltpu.get_barrier_semaphore()
    up = lax.rem(z + 1, nz) * 2 + core
    down = lax.rem(z + nz - 1, nz) * 2 + core
    for d in range(1, n):
        pl.semaphore_signal(
            barrier, inc=1, device_id=(dp, lax.rem(me + d, n)), device_id_type=MESH
        )
    pl.semaphore_signal(barrier, inc=1, device_id=(other, me), device_id_type=MESH)

    @pl.when(z < nz - 1)
    def _():
        pl.semaphore_signal(barrier, inc=1, device_id=(up, me), device_id_type=MESH)

    @pl.when(z > 0)
    def _():
        pl.semaphore_signal(barrier, inc=1, device_id=(down, me), device_id_type=MESH)

    ends = jnp.where(z == 0, 1, 0) + jnp.where(z == nz - 1, 1, 0)
    pl.semaphore_wait(barrier, n - 1 + 3 - ends)

    def partner(d):
        return lax.rem(me + d, n)

    def column(p, h):
        return span(p * heads + h, HEAD_SIZE)

    mine = pl.ds(me * held, held)

    class Trade:
        def __init__(self, src_of, dst, sems, where):
            self.src_of, self.dst = src_of, dst
            self.send, self.recv, self.own_sem = (r[sems + x].at[where] for x in "srl")

        def copy(self, d):
            p = partner(d)
            return pltpu.make_async_remote_copy(
                self.src_of(p), self.dst, self.send.at[d], self.recv.at[d],
                device_id=(dp, p), device_id_type=MESH,
            )

        def own(self):
            return pltpu.make_async_copy(self.src_of(me), self.dst, self.own_sem)

        def start(self):
            for d in range(1, n):
                self.copy(d).start()
            self.own().start()

        def arrive(self):
            self.own().wait()
            for d in range(1, n):
                self.copy(d).wait_recv()

        def sent(self):
            for d in range(1, n):
                self.copy(d).wait_send()

    rows = {
        (t, h): Trade(lambda p, x=x, h=h: x.at[:, :, column(p, h)], r[f"{t}{h}"].at[mine], "in_", (h, i))
        for i, (t, x) in enumerate((("k", k), ("q", q), ("v", v)))
        for h in range(heads)
    }
    cots = [
        Trade(lambda p, h=h: r["cotbuf"].at[h, p], r[f"c{h}"].at[mine], "in_", (h, 3))
        for h in range(heads)
    ]
    attns = [
        Trade(
            lambda p, h=h: r["attn"].at[h, span(p, tokens), :],
            seq.at[h, :, span(me, HEAD_SIZE)], "out_", (h, 0),
        )
        for h in range(heads)
    ]
    grads = {
        (t, h): Trade(
            lambda p, h=h, t=t: r[t].at[h, span(p, tokens), :], o.at[:, column(me, h)], "out_", (h, i)
        )
        for i, t, o in ((1, "dq", dqo), (2, "dk", dko), (3, "dv", dvo))
        for h in range(heads)
    }

    order = [rows[t, h] for h in range(heads) for t in "kqv"]

    def send_rows(first, last):
        for trade in order[first:last]:
            trade.start()

    send_rows(0, 3 + EARLY)
    load_oc = pltpu.make_async_copy(oc, ocv, loc.at[0])
    load_oc.start()
    load_w = []
    for h in range(heads):
        for p in range(n):
            copy = pltpu.make_async_copy(
                w.at[:, pl.ds((p * heads + h) * HEAD_SIZE, HEAD_SIZE)],
                wv.at[h, :, pl.ds(p * HEAD_SIZE, HEAD_SIZE)],
                r["wsem"].at[h, p],
            )
            copy.start()
            load_w.append(copy)

    def place(i, carry):
        def one(b, carry):
            at = empty
            for j in range(chosen):
                at = jnp.where(picks[j, i] == b, i * chosen + j, at)
            pos[i, b] = at
            return carry

        return lax.fori_loop(0, blocks, one, carry)

    lax.fori_loop(0, blocks, place, 0)
    for h in range(heads):
        ps[h, empty] = jnp.zeros((BLOCK_TOKENS, BLOCK_TOKENS), BF16)
    dss[empty] = jnp.zeros((BLOCK_TOKENS, BLOCK_TOKENS), BF16)

    load_oc.wait()

    def flip(i, carry):
        octv[span(i, 256), :] = ocv[:, span(i, 256)].T
        return carry

    lax.fori_loop(0, model // 256, flip, 0)
    for copy in load_w:
        copy.wait()

    def work_cot(h):
        def body(p, carry):
            r["cotbuf"][h, p] = (
                mm(ocv[...], wv[h, :, span(p, HEAD_SIZE)])
                .astype(BF16)
                .reshape(held, BLOCK_TOKENS, HEAD_SIZE)
            )
            return carry

        lax.fori_loop(0, n, body, 0)

    for h in range(heads):
        work_cot(h)

    def listed(ref, i, axis):
        return jnp.concatenate([ref[picks[j, i]] for j in range(chosen)], axis=axis)

    def score_block(h, i):
        st = mm(listed(r[f"k{h}"], i, 0), r[f"q{h}"][i], 1, 1)
        top = jnp.max(st, axis=0, keepdims=True)
        e = jnp.exp2((st - top) * factor)
        inv = 1.0 / jnp.sum(e, axis=0, keepdims=True)
        low = (e * inv).astype(BF16)
        ps[h, pl.ds(i * chosen, chosen)] = low.reshape(chosen, BLOCK_TOKENS, BLOCK_TOKENS)

    def mix_block(h, i):
        low = ps[h, pl.ds(i * chosen, chosen)].reshape(-1, BLOCK_TOKENS)
        a = mm(listed(vt, i, 1), low).astype(BF16)
        r["attn"][h, span(i, BLOCK_TOKENS), :] = a.T

    def backward_block(h, i):
        at = span(i, BLOCK_TOKENS)
        ci = r[f"c{h}"][i]
        dpt = mm(listed(r[f"v{h}"], i, 0), ci, 1, 1)
        dot = jnp.sum(
            (ci.astype(F32) * r["attn"][h, at, :].astype(F32)).T, axis=0, keepdims=True
        )
        parts = []
        for j in range(chosen):
            part = slice(j * BLOCK_TOKENS, (j + 1) * BLOCK_TOKENS)
            ds = (ps[h, i * chosen + j].astype(F32) * (dpt[part] - dot)).astype(BF16)
            dss[i * chosen + j] = ds
            parts.append(ds)
        r["dq"][h, at, :] = (mm(listed(kt, i, 1), jnp.concatenate(parts, axis=0)) * scale).T.astype(BF16)

    def collect_part(h, p):
        def wide(kept):
            return jnp.concatenate(
                [
                    jnp.concatenate([kept(pos[i, p * held + x]) for i in range(blocks)], axis=1)
                    for x in range(held)
                ],
                axis=0,
            )

        at = span(p, tokens)
        pst = wide(lambda slot: ps[h, slot])
        r["dv"][h, at, :] = mm(pst, r[f"c{h}"][...].reshape(-1, HEAD_SIZE)).astype(BF16)
        dst = wide(lambda slot: dss[slot])
        r["dk"][h, at, :] = (mm(dst, r[f"q{h}"][...].reshape(-1, HEAD_SIZE)) * scale).astype(BF16)

    def turn(src, dst):
        def body(b, carry):
            dst[b] = src[b].T
            return carry

        lax.fori_loop(0, blocks, body, 0)

    def by_partner(work, trades, hooks):
        def body(t, carry):
            d = t + 1
            work(partner(d))

            @pl.when(d < n)
            def _():
                for trade in trades:
                    trade.copy(d).start()

            for at, hook in hooks.items():
                pl.when(t == at)(hook)
            return carry

        lax.fori_loop(0, n, body, 0)
        for trade in trades:
            trade.own().start()

    def score(h):
        for t in "kq":
            rows[t, h].arrive()

        def body(p, carry):
            for x in range(held):
                score_block(h, p * held + x)
            return carry

        lax.fori_loop(0, n, body, 0)

    def mix(h):
        rows["v", h].arrive()
        turn(r[f"v{h}"], vt)

        def work(p):
            for x in range(held):
                mix_block(h, p * held + x)

        by_partner(work, [attns[h]], {})

    def backward(h, hooks):
        turn(r[f"k{h}"], kt)
        cots[h].arrive()

        def work(p):
            for x in range(held):
                backward_block(h, p * held + x)

        by_partner(work, [grads["dq", h]], hooks)

    def collect(h, hooks):
        by_partner(lambda p: collect_part(h, p), [grads["dv", h], grads["dk", h]], hooks)

    def term(h, c, who):
        return mm(octv[span(2 * c + who, n * sub), :], seq[h]).reshape(n, sub, -1)

    def core_copy(h, c):
        return pltpu.make_async_remote_copy(
            r["csend"].at[h, c], r["crecv"].at[h, c], r["csem_s"].at[h, c], r["csem_r"].at[h, c],
            device_id=(other, me), device_id_type=MESH,
        )

    def give(h):
        def body(c, carry):
            r["csend"][h, c] = term(h, c, 1 - core).astype(BF16)
            core_copy(h, c).start()
            return carry

        lax.fori_loop(0, nz, body, 0)

        def keep(c, carry):
            acc[h, c] = term(h, c, core)
            return carry

        lax.fori_loop(0, nz, keep, 0)

    def take(h):
        def body(c, carry):
            core_copy(h, c).wait()
            for s in range(n):
                acc[h, c, s] += r["crecv"][h, c, s].astype(F32)
            return carry

        lax.fori_loop(0, nz, body, 0)

    def hop(h, c, s, buf, sem, target):
        return pltpu.make_async_remote_copy(
            r["zsend"].at[h, c, s], r[buf].at[h, c, s], r["zsem"].at[h, c, s],
            r[sem].at[h, c, s], device_id=(target, me), device_id_type=MESH,
        )

    def right(h, c, s):
        return hop(h, c, s, "rrecv", "rsem", up)

    def left(h, c, s):
        return hop(h, c, s, "lrecv", "lsem", down)

    def burst(h, b):
        def one_way(rank, chunk_of, link, buf):
            count = jnp.where(rank == 0, nz - 1 if b == 0 else 0, jnp.where(rank <= b, 1, 0))

            def body(i, carry):
                c = chunk_of(b - rank + i // n)
                s = lax.rem(i, n)

                @pl.when(rank > 0)
                def _():
                    link(h, c, s).wait_recv()
                    acc[h, c, s] += r[buf][h, c, s].astype(F32)

                r["zsend"][h, c, s] = acc[h, c, s].astype(BF16)
                link(h, c, s).start()
                return carry

            lax.fori_loop(0, count * n, body, 0)

        one_way(z, lambda x: nz - 1 - x, right, "rrecv")
        one_way(nz - 1 - z, lambda x: x, left, "lrecv")

    def cross(h, s, slot):
        return pltpu.make_async_remote_copy(
            r["xsend"].at[h, s], r["xrecv"].at[h, slot], r["xsem_s"].at[h, s],
            r["xsem_r"].at[h, slot], device_id=(dp, s), device_id_type=MESH,
        )

    def finish(h):
        def body(s, carry):
            @pl.when(z > 0)
            def _():
                right(h, z, s).wait_recv()
                acc[h, z, s] += r["rrecv"][h, z, s].astype(F32)

            @pl.when(z < nz - 1)
            def _():
                left(h, z, s).wait_recv()
                acc[h, z, s] += r["lrecv"][h, z, s].astype(F32)

            @pl.when(s != me)
            def _():
                r["xsend"][h, s] = acc[h, z, s].astype(BF16)
                cross(h, s, me).start()

            return carry

        lax.fori_loop(0, n, body, 0)

    def total(h):
        r["sum"][...] = acc[h, z, me]

        def body(p, carry):
            @pl.when(p != me)
            def _():
                cross(h, p, p).wait_recv()
                r["sum"][...] += r["xrecv"][h, p].astype(F32)

            return carry

        lax.fori_loop(0, n, body, 0)
        for p in range(n):
            wg[:, pl.ds((p * heads + h) * HEAD_SIZE, HEAD_SIZE)] = r["sum"][
                :, p * HEAD_SIZE : (p + 1) * HEAD_SIZE
            ] * (1.0 / (2 * nz))

    def drain(h):
        def body(s, carry):
            @pl.when(s != me)
            def _():
                cross(h, s, me).wait_send()

            for c in range(nz):
                @pl.when(z < c)
                def _():
                    right(h, c, s).wait_send()

                @pl.when(z > c)
                def _():
                    left(h, c, s).wait_send()

            return carry

        lax.fori_loop(0, n, body, 0)

    tile = 256

    def project():
        def body(i, carry):
            at = span(i, tile)
            part = mm(seq[0], wv[0, at, :], 1, 1)
            for h in range(1, heads):
                part += mm(seq[h], wv[h, at, :], 1, 1)
            out[:, at] = part.astype(BF16)
            return carry

        lax.fori_loop(0, model // tile, body, 0)

    def begin(h):
        take(h)
        burst(h, 0)

    half = n // 2 - 1
    last = n - 1
    score(0)
    mix(0)
    send_rows(3 + EARLY, 6 + EARLY)
    for h in range(1, heads):
        score(h)
        attns[h - 1].arrive()
        give(h - 1)
        cots[h - 1].start()
        mix(h)
        send_rows(3 * h + 3 + EARLY, 3 * h + 6 + EARLY)
        begin(h - 1)
    cots[heads - 1].start()
    for h in range(heads):
        if h == heads - 1:
            attns[h].arrive()
            give(h)
        if h == 0 and heads > 1:
            backward(h, {last: lambda: burst(h, 1)})
        elif h == heads - 1:
            hooks = {half: lambda: begin(h)}
            if h > 0:
                hooks[last] = lambda: finish(h - 1)
            backward(h, hooks)
            if h == 0:
                burst(h, 1)
        else:
            backward(h, {half: lambda: finish(h - 1), last: lambda: burst(h, 1)})
            burst(h, 2)
        if h == heads - 1:
            collect(h, {0: lambda: burst(h, 1), last: lambda: burst(h, 2)} if h > 0 else {last: lambda: burst(h, 2)})
        elif h == 0:
            collect(h, {half: lambda: burst(h, 2)})
        else:
            collect(h, {})
        for b in range(3, nz - 1):
            burst(h, b)
    project()
    finish(heads - 1)
    for h in range(heads):
        total(h)
    for h in range(heads):
        drain(h)
    for trade in grads.values():
        trade.arrive()
    for trade in (*rows.values(), *cots, *attns, *grads.values()):
        trade.sent()


def store_kernel(*refs):
    sems = refs[-1]
    copies = [
        pltpu.make_async_copy(refs[i], refs[5 + i], sems.at[i]) for i in range(5)
    ]
    for copy in copies:
        copy.start()
    for copy in copies:
        copy.wait()


def shards(queries, keys, values, out_weight, out_cot, block_list):
    n = lax.axis_size("ctx")
    n_dp = lax.axis_size("dp")
    nz = n_dp // 2
    _, tokens, total = queries.shape
    model = out_weight.shape[0]
    heads = total // n // HEAD_SIZE
    length = tokens * n
    held = tokens // BLOCK_TOKENS
    blocks, chosen = block_list.shape
    sub = model // (n * n_dp)
    anyspec = pl.BlockSpec(memory_space=pl.ANY)
    vspec = pl.BlockSpec(memory_space=pltpu.VMEM)
    sspec = pl.BlockSpec(memory_space=pltpu.SMEM)
    dma = pltpu.SemaphoreType.DMA

    width = n * HEAD_SIZE
    lane = (heads, nz, n, sub, width)
    cross = (heads, n, sub, width)
    byhead = (heads, length, HEAD_SIZE)
    scratch = {
        "ocv": pltpu.VMEM((tokens, model), BF16),
        "octv": pltpu.VMEM((model, tokens), BF16),
        "wv": pltpu.VMEM((heads, model, width), BF16),
        "seq": pltpu.VMEM((heads, tokens, width), BF16),
        "cotbuf": pltpu.VMEM((heads, n, held, BLOCK_TOKENS, HEAD_SIZE), BF16),
        "attn": pltpu.VMEM(byhead, BF16),
        "dq": pltpu.VMEM(byhead, BF16),
        "dk": pltpu.VMEM(byhead, BF16),
        "dv": pltpu.VMEM(byhead, BF16),
        "ps": pltpu.VMEM((heads, blocks * chosen + 1, BLOCK_TOKENS, BLOCK_TOKENS), BF16),
        "dss": pltpu.VMEM((blocks * chosen + 1, BLOCK_TOKENS, BLOCK_TOKENS), BF16),
        "kt": pltpu.VMEM((blocks, HEAD_SIZE, BLOCK_TOKENS), BF16),
        "vt": pltpu.VMEM((blocks, HEAD_SIZE, BLOCK_TOKENS), BF16),
        "acc": pltpu.VMEM(lane, F32),
        "sum": pltpu.VMEM((sub, width), F32),
        "csend": pltpu.VMEM(lane, BF16),
        "crecv": pltpu.VMEM(lane, BF16),
        "zsend": pltpu.VMEM(lane, BF16),
        "rrecv": pltpu.VMEM(lane, BF16),
        "lrecv": pltpu.VMEM(lane, BF16),
        "xsend": pltpu.VMEM(cross, BF16),
        "xrecv": pltpu.VMEM(cross, BF16),
        "pos": pltpu.SMEM((blocks, blocks), jnp.int32),
        "loc": dma((1,)),
        "wsem": dma((heads, n)),
        "in_s": dma((heads, 4, n)),
        "in_r": dma((heads, 4, n)),
        "in_l": dma((heads, 4)),
        "out_s": dma((heads, 4, n)),
        "out_r": dma((heads, 4, n)),
        "out_l": dma((heads, 4)),
        "csem_s": dma((heads, nz)),
        "csem_r": dma((heads, nz)),
        "zsem": dma((heads, nz, n)),
        "rsem": dma((heads, nz, n)),
        "lsem": dma((heads, nz, n)),
        "xsem_s": dma((heads, n)),
        "xsem_r": dma((heads, n)),
    }
    for h in range(heads):
        for t in "qkvc":
            scratch[f"{t}{h}"] = pltpu.VMEM((blocks, BLOCK_TOKENS, HEAD_SIZE), BF16)
    rows = [x.reshape(held, BLOCK_TOKENS, total) for x in (queries, keys, values)]
    bytoken = jax.ShapeDtypeStruct((tokens, total), BF16)
    results = (
        jax.ShapeDtypeStruct((tokens, model), BF16),
        bytoken,
        bytoken,
        bytoken,
        jax.ShapeDtypeStruct((sub, total), F32),
    )
    held_results = pl.pallas_call(
        functools.partial(layer_kernel, n, nz, heads, tuple(scratch)),
        out_shape=tuple(pltpu.VMEM(x.shape, x.dtype) for x in results),
        in_specs=[sspec] + [anyspec] * 5,
        out_specs=(vspec,) * 5,
        scratch_shapes=list(scratch.values()),
        compiler_params=pltpu.CompilerParams(
            collective_id=0, has_side_effects=True, vmem_limit_bytes=VMEM_BYTES
        ),
    )(block_list.T, *rows, out_weight, out_cot[0])
    out, dq, dk, dv, wg = pl.pallas_call(
        store_kernel,
        out_shape=results,
        in_specs=[vspec] * 5,
        out_specs=(anyspec,) * 5,
        scratch_shapes=[dma((5,))], compiler_params=pltpu.CompilerParams(vmem_limit_bytes=1024 * 1024),
    )(*[pltpu.with_memory_space_constraint(x, pltpu.VMEM) for x in held_results])
    return out[None], dq[None], dk[None], dv[None], wg


def solution(mesh):
    part = P("dp", "ctx", None)
    return jax.shard_map(
        shards,
        mesh=mesh,
        in_specs=(part, part, part, P(), part, P()),
        out_specs=(part, part, part, part, P(("dp", "ctx"), None)),
        check_vma=False,
    )
```

```python
import functools
import math

import jax
import jax.numpy as jnp
from jax import lax
from jax.experimental import pallas as pl
from jax.experimental.pallas import tpu as pltpu
from jax.sharding import PartitionSpec as P

HEAD_SIZE = 128
BLOCK_TOKENS = 128
EARLY = 2
MESH = pl.DeviceIdType.MESH
BF16 = jnp.bfloat16
F32 = jnp.float32
VMEM_BYTES = 52 * 1024 * 1024


def mm(a, b, ca=1, cb=0):
    return lax.dot_general(a, b, (((ca,), (cb,)), ((), ())), preferred_element_type=F32)


def span(i, size):
    return pl.ds(pl.multiple_of(i * size, size), size)


def layer_kernel(n, nz, heads, names, picks, q, k, v, w, oc, out, dqo, dko, dvo, wg, *scratch):
    r = dict(zip(names, scratch))
    me = lax.axis_index("ctx")
    dp = lax.axis_index("dp")
    core = lax.rem(dp, 2)
    other = dp + 1 - 2 * core
    z = dp // 2
    held = q.shape[0]
    tokens = held * BLOCK_TOKENS
    model = w.shape[0]
    chosen, blocks = picks.shape
    sub = wg.shape[0]
    empty = blocks * chosen
    scale = 1.0 / math.sqrt(HEAD_SIZE)
    factor = scale * math.log2(math.e)
    ocv, octv, wv, seq = r["ocv"], r["octv"], r["wv"], r["seq"]
    acc, ps, dss, kt, vt = r["acc"], r["ps"], r["dss"], r["kt"], r["vt"]
    pos, loc = r["pos"], r["loc"]

    barrier = pltpu.get_barrier_semaphore()
    up = lax.rem(z + 1, nz) * 2 + core
    down = lax.rem(z + nz - 1, nz) * 2 + core
    for d in range(1, n):
        pl.semaphore_signal(
            barrier, inc=1, device_id=(dp, lax.rem(me + d, n)), device_id_type=MESH
        )
    pl.semaphore_signal(barrier, inc=1, device_id=(other, me), device_id_type=MESH)

    @pl.when(z < nz - 1)
    def _():
        pl.semaphore_signal(barrier, inc=1, device_id=(up, me), device_id_type=MESH)

    @pl.when(z > 0)
    def _():
        pl.semaphore_signal(barrier, inc=1, device_id=(down, me), device_id_type=MESH)

    ends = jnp.where(z == 0, 1, 0) + jnp.where(z == nz - 1, 1, 0)
    pl.semaphore_wait(barrier, n - 1 + 3 - ends)

    def partner(d):
        return lax.rem(me + d, n)

    def column(p, h):
        return span(p * heads + h, HEAD_SIZE)

    mine = pl.ds(me * held, held)

    class Trade:
        def __init__(self, src_of, dst, sems, where):
            self.src_of, self.dst = src_of, dst
            self.send, self.recv, self.own_sem = (r[sems + x].at[where] for x in "srl")

        def copy(self, d):
            p = partner(d)
            return pltpu.make_async_remote_copy(
                self.src_of(p), self.dst, self.send.at[d], self.recv.at[d],
                device_id=(dp, p), device_id_type=MESH,
            )

        def own(self):
            return pltpu.make_async_copy(self.src_of(me), self.dst, self.own_sem)

        def start(self):
            for d in range(1, n):
                self.copy(d).start()
            self.own().start()

        def arrive(self):
            self.own().wait()
            for d in range(1, n):
                self.copy(d).wait_recv()

        def sent(self):
            for d in range(1, n):
                self.copy(d).wait_send()

    rows = {
        (t, h): Trade(lambda p, x=x, h=h: x.at[:, :, column(p, h)], r[f"{t}{h}"].at[mine], "in_", (h, i))
        for i, (t, x) in enumerate((("k", k), ("q", q), ("v", v)))
        for h in range(heads)
    }
    cots = [
        Trade(lambda p, h=h: r["cotbuf"].at[h, p], r[f"c{h}"].at[mine], "in_", (h, 3))
        for h in range(heads)
    ]
    attns = [
        Trade(
            lambda p, h=h: r["attn"].at[h, span(p, tokens), :],
            seq.at[h, :, span(me, HEAD_SIZE)], "out_", (h, 0),
        )
        for h in range(heads)
    ]
    grads = {
        (t, h): Trade(
            lambda p, h=h, t=t: r[t].at[h, span(p, tokens), :], o.at[:, column(me, h)], "out_", (h, i)
        )
        for i, t, o in ((1, "dq", dqo), (2, "dk", dko), (3, "dv", dvo))
        for h in range(heads)
    }

    order = [rows[t, h] for h in range(heads) for t in "kqv"]

    def send_rows(first, last):
        for trade in order[first:last]:
            trade.start()

    send_rows(0, 3 + EARLY)
    load_oc = pltpu.make_async_copy(oc, ocv, loc.at[0])
    load_oc.start()
    load_w = []
    for h in range(heads):
        for p in range(n):
            copy = pltpu.make_async_copy(
                w.at[:, pl.ds((p * heads + h) * HEAD_SIZE, HEAD_SIZE)],
                wv.at[h, :, pl.ds(p * HEAD_SIZE, HEAD_SIZE)],
                r["wsem"].at[h, p],
            )
            copy.start()
            load_w.append(copy)

    def place(i, carry):
        def one(b, carry):
            at = empty
            for j in range(chosen):
                at = jnp.where(picks[j, i] == b, i * chosen + j, at)
            pos[i, b] = at
            return carry

        return lax.fori_loop(0, blocks, one, carry)

    lax.fori_loop(0, blocks, place, 0)
    for h in range(heads):
        ps[h, empty] = jnp.zeros((BLOCK_TOKENS, BLOCK_TOKENS), BF16)
    dss[empty] = jnp.zeros((BLOCK_TOKENS, BLOCK_TOKENS), BF16)

    load_oc.wait()

    def flip(i, carry):
        octv[span(i, 256), :] = ocv[:, span(i, 256)].T
        return carry

    lax.fori_loop(0, model // 256, flip, 0)
    for copy in load_w:
        copy.wait()

    def work_cot(h):
        def body(p, carry):
            r["cotbuf"][h, p] = (
                mm(ocv[...], wv[h, :, span(p, HEAD_SIZE)])
                .astype(BF16)
                .reshape(held, BLOCK_TOKENS, HEAD_SIZE)
            )
            return carry

        lax.fori_loop(0, n, body, 0)

    for h in range(heads):
        work_cot(h)

    def listed(ref, i, axis):
        return jnp.concatenate([ref[picks[j, i]] for j in range(chosen)], axis=axis)

    def score_block(h, i):
        st = mm(listed(r[f"k{h}"], i, 0), r[f"q{h}"][i], 1, 1)
        top = jnp.max(st, axis=0, keepdims=True)
        e = jnp.exp2((st - top) * factor)
        inv = 1.0 / jnp.sum(e, axis=0, keepdims=True)
        low = (e * inv).astype(BF16)
        ps[h, pl.ds(i * chosen, chosen)] = low.reshape(chosen, BLOCK_TOKENS, BLOCK_TOKENS)

    def mix_block(h, i):
        low = ps[h, pl.ds(i * chosen, chosen)].reshape(-1, BLOCK_TOKENS)
        a = mm(listed(vt, i, 1), low).astype(BF16)
        r["attn"][h, span(i, BLOCK_TOKENS), :] = a.T

    def backward_block(h, i):
        at = span(i, BLOCK_TOKENS)
        ci = r[f"c{h}"][i]
        dpt = mm(listed(r[f"v{h}"], i, 0), ci, 1, 1)
        dot = jnp.sum(
            (ci.astype(F32) * r["attn"][h, at, :].astype(F32)).T, axis=0, keepdims=True
        )
        parts = []
        for j in range(chosen):
            part = slice(j * BLOCK_TOKENS, (j + 1) * BLOCK_TOKENS)
            ds = (ps[h, i * chosen + j].astype(F32) * (dpt[part] - dot)).astype(BF16)
            dss[i * chosen + j] = ds
            parts.append(ds)
        r["dq"][h, at, :] = (mm(listed(kt, i, 1), jnp.concatenate(parts, axis=0)) * scale).T.astype(BF16)

    def collect_part(h, p):
        def wide(kept):
            return jnp.concatenate(
                [
                    jnp.concatenate([kept(pos[i, p * held + x]) for i in range(blocks)], axis=1)
                    for x in range(held)
                ],
                axis=0,
            )

        at = span(p, tokens)
        pst = wide(lambda slot: ps[h, slot])
        r["dv"][h, at, :] = mm(pst, r[f"c{h}"][...].reshape(-1, HEAD_SIZE)).astype(BF16)
        dst = wide(lambda slot: dss[slot])
        r["dk"][h, at, :] = (mm(dst, r[f"q{h}"][...].reshape(-1, HEAD_SIZE)) * scale).astype(BF16)

    def turn(src, dst):
        def body(b, carry):
            dst[b] = src[b].T
            return carry

        lax.fori_loop(0, blocks, body, 0)

    def by_partner(work, trades, hooks):
        def body(t, carry):
            d = t + 1
            work(partner(d))

            @pl.when(d < n)
            def _():
                for trade in trades:
                    trade.copy(d).start()

            for at, hook in hooks.items():
                pl.when(t == at)(hook)
            return carry

        lax.fori_loop(0, n, body, 0)
        for trade in trades:
            trade.own().start()

    def score(h):
        for t in "kq":
            rows[t, h].arrive()

        def body(p, carry):
            for x in range(held):
                score_block(h, p * held + x)
            return carry

        lax.fori_loop(0, n, body, 0)

    def mix(h):
        rows["v", h].arrive()
        turn(r[f"v{h}"], vt)

        def work(p):
            for x in range(held):
                mix_block(h, p * held + x)

        by_partner(work, [attns[h]], {})

    def backward(h, hooks):
        turn(r[f"k{h}"], kt)
        cots[h].arrive()

        def work(p):
            for x in range(held):
                backward_block(h, p * held + x)

        by_partner(work, [grads["dq", h]], hooks)

    def collect(h, hooks):
        by_partner(lambda p: collect_part(h, p), [grads["dv", h], grads["dk", h]], hooks)

    def term(h, c, who):
        return mm(octv[span(2 * c + who, n * sub), :], seq[h]).reshape(n, sub, -1)

    def core_copy(h, c):
        return pltpu.make_async_remote_copy(
            r["csend"].at[h, c], r["crecv"].at[h, c], r["csem_s"].at[h, c], r["csem_r"].at[h, c],
            device_id=(other, me), device_id_type=MESH,
        )

    def give(h):
        def body(c, carry):
            r["csend"][h, c] = term(h, c, 1 - core).astype(BF16)
            core_copy(h, c).start()
            return carry

        lax.fori_loop(0, nz, body, 0)

        def keep(c, carry):
            acc[h, c] = term(h, c, core)
            return carry

        lax.fori_loop(0, nz, keep, 0)

    def take(h):
        def body(c, carry):
            core_copy(h, c).wait()
            for s in range(n):
                acc[h, c, s] += r["crecv"][h, c, s].astype(F32)
            return carry

        lax.fori_loop(0, nz, body, 0)

    def hop(h, c, s, buf, sem, target):
        return pltpu.make_async_remote_copy(
            r["zsend"].at[h, c, s], r[buf].at[h, c, s], r["zsem"].at[h, c, s],
            r[sem].at[h, c, s], device_id=(target, me), device_id_type=MESH,
        )

    def right(h, c, s):
        return hop(h, c, s, "rrecv", "rsem", up)

    def left(h, c, s):
        return hop(h, c, s, "lrecv", "lsem", down)

    def burst(h, b):
        def one_way(rank, chunk_of, link, buf):
            count = jnp.where(rank == 0, nz - 1 if b == 0 else 0, jnp.where(rank <= b, 1, 0))

            def body(i, carry):
                c = chunk_of(b - rank + i // n)
                s = lax.rem(i, n)

                @pl.when(rank > 0)
                def _():
                    link(h, c, s).wait_recv()
                    acc[h, c, s] += r[buf][h, c, s].astype(F32)

                r["zsend"][h, c, s] = acc[h, c, s].astype(BF16)
                link(h, c, s).start()
                return carry

            lax.fori_loop(0, count * n, body, 0)

        one_way(z, lambda x: nz - 1 - x, right, "rrecv")
        one_way(nz - 1 - z, lambda x: x, left, "lrecv")

    def cross(h, s, slot):
        return pltpu.make_async_remote_copy(
            r["xsend"].at[h, s], r["xrecv"].at[h, slot], r["xsem_s"].at[h, s],
            r["xsem_r"].at[h, slot], device_id=(dp, s), device_id_type=MESH,
        )

    def finish(h):
        def body(s, carry):
            @pl.when(z > 0)
            def _():
                right(h, z, s).wait_recv()
                acc[h, z, s] += r["rrecv"][h, z, s].astype(F32)

            @pl.when(z < nz - 1)
            def _():
                left(h, z, s).wait_recv()
                acc[h, z, s] += r["lrecv"][h, z, s].astype(F32)

            @pl.when(s != me)
            def _():
                r["xsend"][h, s] = acc[h, z, s].astype(BF16)
                cross(h, s, me).start()

            return carry

        lax.fori_loop(0, n, body, 0)

    def total(h):
        r["sum"][...] = acc[h, z, me]

        def body(p, carry):
            @pl.when(p != me)
            def _():
                cross(h, p, p).wait_recv()
                r["sum"][...] += r["xrecv"][h, p].astype(F32)

            return carry

        lax.fori_loop(0, n, body, 0)
        for p in range(n):
            wg[:, pl.ds((p * heads + h) * HEAD_SIZE, HEAD_SIZE)] = r["sum"][
                :, p * HEAD_SIZE : (p + 1) * HEAD_SIZE
            ] * (1.0 / (2 * nz))

    def drain(h):
        def body(s, carry):
            @pl.when(s != me)
            def _():
                cross(h, s, me).wait_send()

            for c in range(nz):
                @pl.when(z < c)
                def _():
                    right(h, c, s).wait_send()

                @pl.when(z > c)
                def _():
                    left(h, c, s).wait_send()

            return carry

        lax.fori_loop(0, n, body, 0)

    tile = 256

    def project():
        def body(i, carry):
            at = span(i, tile)
            part = mm(seq[0], wv[0, at, :], 1, 1)
            for h in range(1, heads):
                part += mm(seq[h], wv[h, at, :], 1, 1)
            out[:, at] = part.astype(BF16)
            return carry

        lax.fori_loop(0, model // tile, body, 0)

    def begin(h):
        take(h)
        burst(h, 0)

    half = n // 2 - 1
    last = n - 1
    score(0)
    mix(0)
    send_rows(3 + EARLY, 6 + EARLY)
    for h in range(1, heads):
        score(h)
        attns[h - 1].arrive()
        give(h - 1)
        cots[h - 1].start()
        mix(h)
        send_rows(3 * h + 3 + EARLY, 3 * h + 6 + EARLY)
        begin(h - 1)
    cots[heads - 1].start()
    for h in range(heads):
        if h == 0 and heads == 1:
            attns[h].arrive()
            give(h)
        if h == 0 and heads > 1:
            backward(h, {last: lambda: burst(h, 1)})
            if h == heads - 2:
                attns[h + 1].arrive()
                give(h + 1)
        elif h == heads - 1:
            hooks = {0: lambda: begin(h)}
            if h > 0:
                hooks[last] = lambda: finish(h - 1)
            backward(h, hooks)
            if h == 0:
                burst(h, 1)
        else:
            backward(h, {half: lambda: finish(h - 1), last: lambda: burst(h, 1)})
            burst(h, 2)
            if h == heads - 2:
                attns[h + 1].arrive()
                give(h + 1)
        if h == heads - 1:
            collect(h, {half: lambda: burst(h, 1)} if h > 0 else {last: lambda: burst(h, 2)})
        elif h == 0:
            collect(h, {half: lambda: burst(h, 2)})
        else:
            collect(h, {})
        for b in range(3, nz - 1):
            if h == 0 or h + 1 < heads:
                burst(h, b)
    project()
    if heads > 1:
        for b in range(2, nz - 1):
            burst(heads - 1, b)
    finish(heads - 1)
    for h in range(heads):
        total(h)
    for h in range(heads):
        drain(h)
    for trade in grads.values():
        trade.arrive()
    for trade in (*rows.values(), *cots, *attns, *grads.values()):
        trade.sent()


def store_kernel(*refs):
    sems = refs[-1]
    copies = [
        pltpu.make_async_copy(refs[i], refs[5 + i], sems.at[i]) for i in range(5)
    ]
    for copy in copies:
        copy.start()
    for copy in copies:
        copy.wait()


def shards(queries, keys, values, out_weight, out_cot, block_list):
    n = lax.axis_size("ctx")
    n_dp = lax.axis_size("dp")
    nz = n_dp // 2
    _, tokens, total = queries.shape
    model = out_weight.shape[0]
    heads = total // n // HEAD_SIZE
    length = tokens * n
    held = tokens // BLOCK_TOKENS
    blocks, chosen = block_list.shape
    sub = model // (n * n_dp)
    anyspec = pl.BlockSpec(memory_space=pl.ANY)
    vspec = pl.BlockSpec(memory_space=pltpu.VMEM)
    sspec = pl.BlockSpec(memory_space=pltpu.SMEM)
    dma = pltpu.SemaphoreType.DMA

    width = n * HEAD_SIZE
    lane = (heads, nz, n, sub, width)
    cross = (heads, n, sub, width)
    byhead = (heads, length, HEAD_SIZE)
    scratch = {
        "ocv": pltpu.VMEM((tokens, model), BF16),
        "octv": pltpu.VMEM((model, tokens), BF16),
        "wv": pltpu.VMEM((heads, model, width), BF16),
        "seq": pltpu.VMEM((heads, tokens, width), BF16),
        "cotbuf": pltpu.VMEM((heads, n, held, BLOCK_TOKENS, HEAD_SIZE), BF16),
        "attn": pltpu.VMEM(byhead, BF16),
        "dq": pltpu.VMEM(byhead, BF16),
        "dk": pltpu.VMEM(byhead, BF16),
        "dv": pltpu.VMEM(byhead, BF16),
        "ps": pltpu.VMEM((heads, blocks * chosen + 1, BLOCK_TOKENS, BLOCK_TOKENS), BF16),
        "dss": pltpu.VMEM((blocks * chosen + 1, BLOCK_TOKENS, BLOCK_TOKENS), BF16),
        "kt": pltpu.VMEM((blocks, HEAD_SIZE, BLOCK_TOKENS), BF16),
        "vt": pltpu.VMEM((blocks, HEAD_SIZE, BLOCK_TOKENS), BF16),
        "acc": pltpu.VMEM(lane, F32),
        "sum": pltpu.VMEM((sub, width), F32),
        "csend": pltpu.VMEM(lane, BF16),
        "crecv": pltpu.VMEM(lane, BF16),
        "zsend": pltpu.VMEM(lane, BF16),
        "rrecv": pltpu.VMEM(lane, BF16),
        "lrecv": pltpu.VMEM(lane, BF16),
        "xsend": pltpu.VMEM(cross, BF16),
        "xrecv": pltpu.VMEM(cross, BF16),
        "pos": pltpu.SMEM((blocks, blocks), jnp.int32),
        "loc": dma((1,)),
        "wsem": dma((heads, n)),
        "in_s": dma((heads, 4, n)),
        "in_r": dma((heads, 4, n)),
        "in_l": dma((heads, 4)),
        "out_s": dma((heads, 4, n)),
        "out_r": dma((heads, 4, n)),
        "out_l": dma((heads, 4)),
        "csem_s": dma((heads, nz)),
        "csem_r": dma((heads, nz)),
        "zsem": dma((heads, nz, n)),
        "rsem": dma((heads, nz, n)),
        "lsem": dma((heads, nz, n)),
        "xsem_s": dma((heads, n)),
        "xsem_r": dma((heads, n)),
    }
    for h in range(heads):
        for t in "qkvc":
            scratch[f"{t}{h}"] = pltpu.VMEM((blocks, BLOCK_TOKENS, HEAD_SIZE), BF16)
    rows = [x.reshape(held, BLOCK_TOKENS, total) for x in (queries, keys, values)]
    bytoken = jax.ShapeDtypeStruct((tokens, total), BF16)
    results = (
        jax.ShapeDtypeStruct((tokens, model), BF16),
        bytoken,
        bytoken,
        bytoken,
        jax.ShapeDtypeStruct((sub, total), F32),
    )
    held_results = pl.pallas_call(
        functools.partial(layer_kernel, n, nz, heads, tuple(scratch)),
        out_shape=tuple(pltpu.VMEM(x.shape, x.dtype) for x in results),
        in_specs=[sspec] + [anyspec] * 5,
        out_specs=(vspec,) * 5,
        scratch_shapes=list(scratch.values()),
        compiler_params=pltpu.CompilerParams(
            collective_id=0, has_side_effects=True, vmem_limit_bytes=VMEM_BYTES
        ),
    )(block_list.T, *rows, out_weight, out_cot[0])
    out, dq, dk, dv, wg = pl.pallas_call(
        store_kernel,
        out_shape=results,
        in_specs=[vspec] * 5,
        out_specs=(anyspec,) * 5,
        scratch_shapes=[dma((5,))], compiler_params=pltpu.CompilerParams(vmem_limit_bytes=1024 * 1024),
    )(*[pltpu.with_memory_space_constraint(x, pltpu.VMEM) for x in held_results])
    return out[None], dq[None], dk[None], dv[None], wg


def solution(mesh):
    part = P("dp", "ctx", None)
    return jax.shard_map(
        shards,
        mesh=mesh,
        in_specs=(part, part, part, P(), part, P()),
        out_specs=(part, part, part, part, P(("dp", "ctx"), None)),
        check_vma=False,
    )
```

```python
import functools
import math

import jax
import jax.numpy as jnp
from jax import lax
from jax.experimental import pallas as pl
from jax.experimental.pallas import tpu as pltpu
from jax.sharding import PartitionSpec as P

HEAD_SIZE = 128
BLOCK_TOKENS = 128
EARLY = 2
MESH = pl.DeviceIdType.MESH
BF16 = jnp.bfloat16
F32 = jnp.float32
VMEM_BYTES = 52 * 1024 * 1024


def mm(a, b, ca=1, cb=0):
    return lax.dot_general(a, b, (((ca,), (cb,)), ((), ())), preferred_element_type=F32)


def span(i, size):
    return pl.ds(pl.multiple_of(i * size, size), size)


def layer_kernel(n, nz, heads, names, picks, q, k, v, w, oc, out, dqo, dko, dvo, wg, *scratch):
    r = dict(zip(names, scratch))
    me = lax.axis_index("ctx")
    dp = lax.axis_index("dp")
    core = lax.rem(dp, 2)
    other = dp + 1 - 2 * core
    z = dp // 2
    held = q.shape[0]
    tokens = held * BLOCK_TOKENS
    model = w.shape[0]
    chosen, blocks = picks.shape
    sub = wg.shape[0]
    empty = blocks * chosen
    scale = 1.0 / math.sqrt(HEAD_SIZE)
    factor = scale * math.log2(math.e)
    ocv, octv, wv, seq = r["ocv"], r["octv"], r["wv"], r["seq"]
    acc, ps, dss, kt, vt = r["acc"], r["ps"], r["dss"], r["kt"], r["vt"]
    pos, loc = r["pos"], r["loc"]

    barrier = pltpu.get_barrier_semaphore()
    up = lax.rem(z + 1, nz) * 2 + core
    down = lax.rem(z + nz - 1, nz) * 2 + core
    for d in range(1, n):
        pl.semaphore_signal(
            barrier, inc=1, device_id=(dp, lax.rem(me + d, n)), device_id_type=MESH
        )
    pl.semaphore_signal(barrier, inc=1, device_id=(other, me), device_id_type=MESH)

    @pl.when(z < nz - 1)
    def _():
        pl.semaphore_signal(barrier, inc=1, device_id=(up, me), device_id_type=MESH)

    @pl.when(z > 0)
    def _():
        pl.semaphore_signal(barrier, inc=1, device_id=(down, me), device_id_type=MESH)

    ends = jnp.where(z == 0, 1, 0) + jnp.where(z == nz - 1, 1, 0)
    pl.semaphore_wait(barrier, n - 1 + 3 - ends)

    def partner(d):
        return lax.rem(me + d, n)

    def column(p, h):
        return span(p * heads + h, HEAD_SIZE)

    mine = pl.ds(me * held, held)

    class Trade:
        def __init__(self, src_of, dst, sems, where):
            self.src_of, self.dst = src_of, dst
            self.send, self.recv, self.own_sem = (r[sems + x].at[where] for x in "srl")

        def copy(self, d):
            p = partner(d)
            return pltpu.make_async_remote_copy(
                self.src_of(p), self.dst, self.send.at[d], self.recv.at[d],
                device_id=(dp, p), device_id_type=MESH,
            )

        def own(self):
            return pltpu.make_async_copy(self.src_of(me), self.dst, self.own_sem)

        def start(self):
            for d in range(1, n):
                self.copy(d).start()
            self.own().start()

        def arrive(self):
            self.own().wait()
            for d in range(1, n):
                self.copy(d).wait_recv()

        def sent(self):
            for d in range(1, n):
                self.copy(d).wait_send()

    rows = {
        (t, h): Trade(lambda p, x=x, h=h: x.at[:, :, column(p, h)], r[f"{t}{h}"].at[mine], "in_", (h, i))
        for i, (t, x) in enumerate((("k", k), ("q", q), ("v", v)))
        for h in range(heads)
    }
    cots = [
        Trade(lambda p, h=h: r["cotbuf"].at[h, p], r[f"c{h}"].at[mine], "in_", (h, 3))
        for h in range(heads)
    ]
    attns = [
        Trade(
            lambda p, h=h: r["attn"].at[h, span(p, tokens), :],
            seq.at[h, :, span(me, HEAD_SIZE)], "out_", (h, 0),
        )
        for h in range(heads)
    ]
    grads = {
        (t, h): Trade(
            lambda p, h=h, t=t: r[t].at[h, span(p, tokens), :], o.at[:, column(me, h)], "out_", (h, i)
        )
        for i, t, o in ((1, "dq", dqo), (2, "dk", dko), (3, "dv", dvo))
        for h in range(heads)
    }

    order = [rows[t, h] for h in range(heads) for t in "kqv"]

    def send_rows(first, last):
        for trade in order[first:last]:
            trade.start()

    send_rows(0, 3 + EARLY)
    load_oc = pltpu.make_async_copy(oc, ocv, loc.at[0])
    load_oc.start()
    load_w = []
    for h in range(heads):
        for p in range(n):
            copy = pltpu.make_async_copy(
                w.at[:, pl.ds((p * heads + h) * HEAD_SIZE, HEAD_SIZE)],
                wv.at[h, :, pl.ds(p * HEAD_SIZE, HEAD_SIZE)],
                r["wsem"].at[h, p],
            )
            copy.start()
            load_w.append(copy)

    def place(i, carry):
        def one(b, carry):
            at = empty
            for j in range(chosen):
                at = jnp.where(picks[j, i] == b, i * chosen + j, at)
            pos[i, b] = at
            return carry

        return lax.fori_loop(0, blocks, one, carry)

    lax.fori_loop(0, blocks, place, 0)
    for h in range(heads):
        ps[h, empty] = jnp.zeros((BLOCK_TOKENS, BLOCK_TOKENS), BF16)
    dss[empty] = jnp.zeros((BLOCK_TOKENS, BLOCK_TOKENS), BF16)

    load_oc.wait()

    def flip(i, carry):
        octv[span(i, 256), :] = ocv[:, span(i, 256)].T
        return carry

    lax.fori_loop(0, model // 256, flip, 0)
    for copy in load_w:
        copy.wait()

    def work_cot(h):
        def body(p, carry):
            r["cotbuf"][h, p] = (
                mm(ocv[...], wv[h, :, span(p, HEAD_SIZE)])
                .astype(BF16)
                .reshape(held, BLOCK_TOKENS, HEAD_SIZE)
            )
            return carry

        lax.fori_loop(0, n, body, 0)

    for h in range(heads):
        work_cot(h)

    def listed(ref, i, axis):
        return jnp.concatenate([ref[picks[j, i]] for j in range(chosen)], axis=axis)

    def score_block(h, i):
        st = mm(listed(r[f"k{h}"], i, 0), r[f"q{h}"][i], 1, 1)
        top = jnp.max(st, axis=0, keepdims=True)
        e = jnp.exp2((st - top) * factor)
        inv = 1.0 / jnp.sum(e, axis=0, keepdims=True)
        low = (e * inv).astype(BF16)
        ps[h, pl.ds(i * chosen, chosen)] = low.reshape(chosen, BLOCK_TOKENS, BLOCK_TOKENS)

    def mix_block(h, i):
        low = ps[h, pl.ds(i * chosen, chosen)].reshape(-1, BLOCK_TOKENS)
        a = mm(listed(vt, i, 1), low).astype(BF16)
        r["attn"][h, span(i, BLOCK_TOKENS), :] = a.T

    def backward_block(h, i):
        at = span(i, BLOCK_TOKENS)
        ci = r[f"c{h}"][i]
        dpt = mm(listed(r[f"v{h}"], i, 0), ci, 1, 1)
        dot = jnp.sum(
            (ci.astype(F32) * r["attn"][h, at, :].astype(F32)).T, axis=0, keepdims=True
        )
        parts = []
        for j in range(chosen):
            part = slice(j * BLOCK_TOKENS, (j + 1) * BLOCK_TOKENS)
            ds = (ps[h, i * chosen + j].astype(F32) * (dpt[part] - dot)).astype(BF16)
            dss[i * chosen + j] = ds
            parts.append(ds)
        r["dq"][h, at, :] = (mm(listed(kt, i, 1), jnp.concatenate(parts, axis=0)) * scale).T.astype(BF16)

    def collect_part(h, p):
        def wide(kept):
            return jnp.concatenate(
                [
                    jnp.concatenate([kept(pos[i, p * held + x]) for i in range(blocks)], axis=1)
                    for x in range(held)
                ],
                axis=0,
            )

        at = span(p, tokens)
        pst = wide(lambda slot: ps[h, slot])
        r["dv"][h, at, :] = mm(pst, r[f"c{h}"][...].reshape(-1, HEAD_SIZE)).astype(BF16)
        dst = wide(lambda slot: dss[slot])
        r["dk"][h, at, :] = (mm(dst, r[f"q{h}"][...].reshape(-1, HEAD_SIZE)) * scale).astype(BF16)

    def turn(src, dst):
        def body(b, carry):
            dst[b] = src[b].T
            return carry

        lax.fori_loop(0, blocks, body, 0)

    def by_partner(work, trades, hooks):
        def body(t, carry):
            d = t + 1
            work(partner(d))

            @pl.when(d < n)
            def _():
                for trade in trades:
                    trade.copy(d).start()

            for at, hook in hooks.items():
                pl.when(t == at)(hook)
            return carry

        lax.fori_loop(0, n, body, 0)
        for trade in trades:
            trade.own().start()

    def score(h):
        for t in "kq":
            rows[t, h].arrive()

        def body(p, carry):
            for x in range(held):
                score_block(h, p * held + x)
            return carry

        lax.fori_loop(0, n, body, 0)

    def mix(h):
        rows["v", h].arrive()
        turn(r[f"v{h}"], vt)

        def work(p):
            for x in range(held):
                mix_block(h, p * held + x)

        by_partner(work, [attns[h]], {})

    def backward(h, hooks):
        turn(r[f"k{h}"], kt)
        cots[h].arrive()

        def work(p):
            for x in range(held):
                backward_block(h, p * held + x)

        by_partner(work, [grads["dq", h]], hooks)

    def collect(h, hooks):
        by_partner(lambda p: collect_part(h, p), [grads["dv", h], grads["dk", h]], hooks)

    def term(h, c, who):
        return mm(octv[span(2 * c + who, n * sub), :], seq[h]).reshape(n, sub, -1)

    def core_copy(h, c):
        return pltpu.make_async_remote_copy(
            r["csend"].at[h, c], r["crecv"].at[h, c], r["csem_s"].at[h, c], r["csem_r"].at[h, c],
            device_id=(other, me), device_id_type=MESH,
        )

    def give(h):
        def body(c, carry):
            r["csend"][h, c] = term(h, c, 1 - core).astype(BF16)
            core_copy(h, c).start()
            return carry

        lax.fori_loop(0, nz, body, 0)

        def keep(c, carry):
            acc[h, c] = term(h, c, core)
            return carry

        lax.fori_loop(0, nz, keep, 0)

    def take(h):
        def body(c, carry):
            core_copy(h, c).wait()
            for s in range(n):
                acc[h, c, s] += r["crecv"][h, c, s].astype(F32)
            return carry

        lax.fori_loop(0, nz, body, 0)

    def hop(h, c, s, buf, sem, target):
        return pltpu.make_async_remote_copy(
            r["zsend"].at[h, c, s], r[buf].at[h, c, s], r["zsem"].at[h, c, s],
            r[sem].at[h, c, s], device_id=(target, me), device_id_type=MESH,
        )

    def right(h, c, s):
        return hop(h, c, s, "rrecv", "rsem", up)

    def left(h, c, s):
        return hop(h, c, s, "lrecv", "lsem", down)

    def burst(h, b):
        def one_way(rank, chunk_of, link, buf):
            count = jnp.where(rank == 0, nz - 1 if b == 0 else 0, jnp.where(rank <= b, 1, 0))

            def body(i, carry):
                c = chunk_of(b - rank + i // n)
                s = lax.rem(i, n)

                @pl.when(rank > 0)
                def _():
                    link(h, c, s).wait_recv()
                    acc[h, c, s] += r[buf][h, c, s].astype(F32)

                r["zsend"][h, c, s] = acc[h, c, s].astype(BF16)
                link(h, c, s).start()
                return carry

            lax.fori_loop(0, count * n, body, 0)

        one_way(z, lambda x: nz - 1 - x, right, "rrecv")
        one_way(nz - 1 - z, lambda x: x, left, "lrecv")

    def cross(h, s, slot):
        return pltpu.make_async_remote_copy(
            r["xsend"].at[h, s], r["xrecv"].at[h, slot], r["xsem_s"].at[h, s],
            r["xsem_r"].at[h, slot], device_id=(dp, s), device_id_type=MESH,
        )

    def finish(h):
        def body(s, carry):
            @pl.when(z > 0)
            def _():
                right(h, z, s).wait_recv()
                acc[h, z, s] += r["rrecv"][h, z, s].astype(F32)

            @pl.when(z < nz - 1)
            def _():
                left(h, z, s).wait_recv()
                acc[h, z, s] += r["lrecv"][h, z, s].astype(F32)

            @pl.when(s != me)
            def _():
                r["xsend"][h, s] = acc[h, z, s].astype(BF16)
                cross(h, s, me).start()

            return carry

        lax.fori_loop(0, n, body, 0)

    def total(h):
        r["sum"][...] = acc[h, z, me]

        def body(p, carry):
            @pl.when(p != me)
            def _():
                cross(h, p, p).wait_recv()
                r["sum"][...] += r["xrecv"][h, p].astype(F32)

            return carry

        lax.fori_loop(0, n, body, 0)
        for p in range(n):
            wg[:, pl.ds((p * heads + h) * HEAD_SIZE, HEAD_SIZE)] = r["sum"][
                :, p * HEAD_SIZE : (p + 1) * HEAD_SIZE
            ] * (1.0 / (2 * nz))

    def drain(h):
        def body(s, carry):
            @pl.when(s != me)
            def _():
                cross(h, s, me).wait_send()

            for c in range(nz):
                @pl.when(z < c)
                def _():
                    right(h, c, s).wait_send()

                @pl.when(z > c)
                def _():
                    left(h, c, s).wait_send()

            return carry

        lax.fori_loop(0, n, body, 0)

    tile = 256

    def project():
        def body(i, carry):
            at = span(i, tile)
            part = mm(seq[0], wv[0, at, :], 1, 1)
            for h in range(1, heads):
                part += mm(seq[h], wv[h, at, :], 1, 1)
            out[:, at] = part.astype(BF16)
            return carry

        lax.fori_loop(0, model // tile, body, 0)

    def begin(h):
        take(h)
        burst(h, 0)

    half = n // 2 - 1
    last = n - 1
    score(0)
    mix(0)
    send_rows(3 + EARLY, 6 + EARLY)
    for h in range(1, heads):
        score(h)
        attns[h - 1].arrive()
        give(h - 1)
        cots[h - 1].start()
        mix(h)
        send_rows(3 * h + 3 + EARLY, 3 * h + 6 + EARLY)
        begin(h - 1)
    cots[heads - 1].start()
    for h in range(heads):
        if h == 0 and heads == 1:
            attns[h].arrive()
            give(h)
        if h == 0 and heads > 1:
            backward(h, {last: lambda: burst(h, 1)})
            if h == heads - 2:
                attns[h + 1].arrive()
                give(h + 1)
        elif h == heads - 1:
            hooks = {0: lambda: begin(h)}
            if h > 0:
                hooks[last] = lambda: finish(h - 1)
            backward(h, hooks)
            if h == 0:
                burst(h, 1)
        else:
            backward(h, {half: lambda: finish(h - 1), last: lambda: burst(h, 1)})
            burst(h, 2)
            if h == heads - 2:
                attns[h + 1].arrive()
                give(h + 1)
        if h == heads - 1:
            collect(h, {half: lambda: burst(h, 1)} if h > 0 else {last: lambda: burst(h, 2)})
        elif h == 0:
            collect(h, {half: lambda: burst(h, 2)})
        else:
            collect(h, {})
        for b in range(3, nz - 1):
            if h == 0 or h + 1 < heads:
                burst(h, b)
    project()
    if heads > 1:
        for b in range(2, nz - 1):
            burst(heads - 1, b)
    for trade in (*rows.values(), *cots, *attns):
        trade.sent()
    for h in range(heads - 1):
        total(h)
        drain(h)
    finish(heads - 1)
    total(heads - 1)
    drain(heads - 1)
    for trade in grads.values():
        trade.arrive()
    for trade in grads.values():
        trade.sent()


def store_kernel(*refs):
    sems = refs[-1]
    copies = [
        pltpu.make_async_copy(refs[i], refs[5 + i], sems.at[i]) for i in range(5)
    ]
    for copy in copies:
        copy.start()
    for copy in copies:
        copy.wait()


def shards(queries, keys, values, out_weight, out_cot, block_list):
    n = lax.axis_size("ctx")
    n_dp = lax.axis_size("dp")
    nz = n_dp // 2
    _, tokens, total = queries.shape
    model = out_weight.shape[0]
    heads = total // n // HEAD_SIZE
    length = tokens * n
    held = tokens // BLOCK_TOKENS
    blocks, chosen = block_list.shape
    sub = model // (n * n_dp)
    anyspec = pl.BlockSpec(memory_space=pl.ANY)
    vspec = pl.BlockSpec(memory_space=pltpu.VMEM)
    sspec = pl.BlockSpec(memory_space=pltpu.SMEM)
    dma = pltpu.SemaphoreType.DMA

    width = n * HEAD_SIZE
    lane = (heads, nz, n, sub, width)
    cross = (heads, n, sub, width)
    byhead = (heads, length, HEAD_SIZE)
    scratch = {
        "ocv": pltpu.VMEM((tokens, model), BF16),
        "octv": pltpu.VMEM((model, tokens), BF16),
        "wv": pltpu.VMEM((heads, model, width), BF16),
        "seq": pltpu.VMEM((heads, tokens, width), BF16),
        "cotbuf": pltpu.VMEM((heads, n, held, BLOCK_TOKENS, HEAD_SIZE), BF16),
        "attn": pltpu.VMEM(byhead, BF16),
        "dq": pltpu.VMEM(byhead, BF16),
        "dk": pltpu.VMEM(byhead, BF16),
        "dv": pltpu.VMEM(byhead, BF16),
        "ps": pltpu.VMEM((heads, blocks * chosen + 1, BLOCK_TOKENS, BLOCK_TOKENS), BF16),
        "dss": pltpu.VMEM((blocks * chosen + 1, BLOCK_TOKENS, BLOCK_TOKENS), BF16),
        "kt": pltpu.VMEM((blocks, HEAD_SIZE, BLOCK_TOKENS), BF16),
        "vt": pltpu.VMEM((blocks, HEAD_SIZE, BLOCK_TOKENS), BF16),
        "acc": pltpu.VMEM(lane, F32),
        "sum": pltpu.VMEM((sub, width), F32),
        "csend": pltpu.VMEM(lane, BF16),
        "crecv": pltpu.VMEM(lane, BF16),
        "zsend": pltpu.VMEM(lane, BF16),
        "rrecv": pltpu.VMEM(lane, BF16),
        "lrecv": pltpu.VMEM(lane, BF16),
        "xsend": pltpu.VMEM(cross, BF16),
        "xrecv": pltpu.VMEM(cross, BF16),
        "pos": pltpu.SMEM((blocks, blocks), jnp.int32),
        "loc": dma((1,)),
        "wsem": dma((heads, n)),
        "in_s": dma((heads, 4, n)),
        "in_r": dma((heads, 4, n)),
        "in_l": dma((heads, 4)),
        "out_s": dma((heads, 4, n)),
        "out_r": dma((heads, 4, n)),
        "out_l": dma((heads, 4)),
        "csem_s": dma((heads, nz)),
        "csem_r": dma((heads, nz)),
        "zsem": dma((heads, nz, n)),
        "rsem": dma((heads, nz, n)),
        "lsem": dma((heads, nz, n)),
        "xsem_s": dma((heads, n)),
        "xsem_r": dma((heads, n)),
    }
    for h in range(heads):
        for t in "qkvc":
            scratch[f"{t}{h}"] = pltpu.VMEM((blocks, BLOCK_TOKENS, HEAD_SIZE), BF16)
    rows = [x.reshape(held, BLOCK_TOKENS, total) for x in (queries, keys, values)]
    bytoken = jax.ShapeDtypeStruct((tokens, total), BF16)
    results = (
        jax.ShapeDtypeStruct((tokens, model), BF16),
        bytoken,
        bytoken,
        bytoken,
        jax.ShapeDtypeStruct((sub, total), F32),
    )
    held_results = pl.pallas_call(
        functools.partial(layer_kernel, n, nz, heads, tuple(scratch)),
        out_shape=tuple(pltpu.VMEM(x.shape, x.dtype) for x in results),
        in_specs=[sspec] + [anyspec] * 5,
        out_specs=(vspec,) * 5,
        scratch_shapes=list(scratch.values()),
        compiler_params=pltpu.CompilerParams(
            collective_id=0, has_side_effects=True, vmem_limit_bytes=VMEM_BYTES
        ),
    )(block_list.T, *rows, out_weight, out_cot[0])
    out, dq, dk, dv, wg = pl.pallas_call(
        store_kernel,
        out_shape=results,
        in_specs=[vspec] * 5,
        out_specs=(anyspec,) * 5,
        scratch_shapes=[dma((5,))], compiler_params=pltpu.CompilerParams(vmem_limit_bytes=1024 * 1024),
    )(*[pltpu.with_memory_space_constraint(x, pltpu.VMEM) for x in held_results])
    return out[None], dq[None], dk[None], dv[None], wg


def solution(mesh):
    part = P("dp", "ctx", None)
    return jax.shard_map(
        shards,
        mesh=mesh,
        in_specs=(part, part, part, P(), part, P()),
        out_specs=(part, part, part, part, P(("dp", "ctx"), None)),
        check_vma=False,
    )
```
